32 devices in a mesh: grp: 4 (over z), wide: 8 (over y, x, core).
Axes of the slice: x: 2, y: 2, z: 4, core: 2. Of those that a mesh axis runs over, the one named last changes fastest.
Arguments:
- coeff_in: float32 [2336, 512], P(('grp', 'wide')), may hold values from -6 to 6
- coupling: float32 [2048, 64, 64], P(('grp', 'wide')), may hold values from -0.5 to 0.5
- source: int32 [2048], P(('grp', 'wide')), may hold values from 0 to 291, as said below
- target: int32 [2048], P(('grp', 'wide')), may hold values from 0 to 72, as said below
- counts: int32 [256], P(('grp', 'wide')), may hold values from 1 to 8, as said below
- transfer: float32 [2304, 64, 64], P(('grp', 'wide')), may hold values from -0.75 to 0.75
- basis: float32 [2048, 64, 128], P(('grp', 'wide')), may hold values from -0.75 to 0.75
Outputs:
- product: float32 [8, 262144], P(None, ('grp', 'wide'))
The draws below stay inside these ranges and needn't reach their ends.
Inputs may be any that keep to these rules, and one draw needn't show every extreme that they name: source names a cluster of the same level as the block's target: member v // 73 of the block's group, local number v % 73. target is the local number of a cluster at the owner. `counts`: in every draw, for each index of grp one index of wide receives 8 live blocks from every device.
All inputs are finite; a program needn't handle non-finite values.
Results may differ from the reference program's by a relative error of at most 0.00007.
Values sent between devices are 32-bit elements; how exact they have to be, the bound alone decides.
No kernel may reach another device: no remote copies, remote signals or barrier semaphores. Data moves between devices by JAX's collectives and lax.ppermute only.
A program may use at most 64 MiB of HBM per device.

```python
import jax
import jax.numpy as jnp
from jax import lax

K = 64
R = 8
BRANCH = 8
LEAF = 128
SLOTS = 8
NCL = 73
BLOCKS = 64
CLUSTERS = 2336
NPTS = 262144
N_GRP = 4
N_WIDE = 8


def block_levels(key):
    total = N_GRP * N_WIDE * N_WIDE * SLOTS
    level = jax.random.randint(jax.random.fold_in(key, 101), (total,), 0, 3)
    offset = jnp.where(level == 0, 0, jnp.where(level == 1, 1, 1 + BRANCH))
    span = jnp.where(level == 0, 1, jnp.where(level == 1, BRANCH, BRANCH * BRANCH))
    return (offset, span)


def draw_source(key, part):
    offset, span = block_levels(key)
    key = jax.random.fold_in(key, 3)
    member = jax.random.randint(jax.random.fold_in(key, 1), offset.shape, 0, N_GRP)
    within = jax.random.randint(jax.random.fold_in(key, 2), offset.shape, 0, span)
    return (member * NCL + offset + within).astype(jnp.int32)


def draw_target(key, part):
    offset, span = block_levels(key)
    key = jax.random.fold_in(key, 4)
    within = jax.random.randint(key, offset.shape, 0, span)
    return (offset + within).astype(jnp.int32)


def draw_counts(key, part):
    key = jax.random.fold_in(key, 5)
    base = jax.random.randint(jax.random.fold_in(key, 1), (N_GRP, N_WIDE, N_WIDE), 1, SLOTS + 1)
    star = jax.random.randint(jax.random.fold_in(key, 2), (N_GRP, 1, 1), 0, N_WIDE)
    full = jnp.arange(N_WIDE)[None, None, :] == star
    return jnp.where(full, SLOTS, base).reshape(-1).astype(jnp.int32)


def steps_of(stream_key, shape, split, smallest, top_value):
    def one(axis_at, blocks):
        draws = jax.random.uniform(jax.random.fold_in(jax.random.fold_in(stream_key, 6), axis_at), (blocks,), jnp.float32, smallest / len(split), top_value / len(split))
        return jnp.repeat(jnp.exp(draws), shape[axis_at] // blocks).reshape((-1,) + (1,) * (len(shape) - axis_at - 1))

    factor_of = one(*split[0])
    for cut in split[1:]:
        factor_of = factor_of * one(*cut)
    return factor_of


def normal_values(stream_key, extent, deviation, limit, split=(), held_as=jnp.bfloat16):
    result = deviation * jax.random.normal(stream_key, extent, jnp.float32)
    if split:
        result = result * steps_of(stream_key, extent, split, -0.22, 0.18)
    return jnp.clip(result, -limit, limit).astype(held_as)


def setup_inputs(seed: int = 0) -> dict:
    key_of = jax.random.split(jax.random.key(seed), 8)
    coeff_in = normal_values(key_of[0], (CLUSTERS, K * R), 1.0, 6.0, ((0, 32),), jnp.float32)
    coupling = normal_values(key_of[1], (N_GRP * N_WIDE * BLOCKS, K, K), (2 * K) ** -0.5, 0.5, ((0, 32),), jnp.float32)
    source = draw_source(jax.random.fold_in(key_of[7], 71), 0)
    target = draw_target(jax.random.fold_in(key_of[7], 71), 0)
    counts = draw_counts(jax.random.fold_in(key_of[7], 71), 0)
    transfer = normal_values(key_of[5], (N_GRP * N_WIDE * (NCL - 1), K, K), K ** -0.5, 0.75, ((0, 32),), jnp.float32)
    basis = normal_values(key_of[6], (N_GRP * N_WIDE * BRANCH * BRANCH, K, LEAF), K ** -0.5, 0.75, ((0, 32),), jnp.float32)
    return {"coeff_in": coeff_in, "coupling": coupling, "source": source, "target": target, "counts": counts, "transfer": transfer, "basis": basis}


def reference(coeff_in, coupling, source, target, counts, transfer, basis):
    ndev = N_GRP * N_WIDE
    blocks = N_WIDE * SLOTS
    idx = jnp.arange(ndev * blocks, dtype=jnp.int32)
    dev = idx // blocks
    loc = idx % blocks
    peer = loc // SLOTS
    slot = loc % SLOTS
    grp_i = dev // N_WIDE
    wide_i = dev % N_WIDE
    src_row = ((source // NCL) * N_WIDE + wide_i) * NCL + source % NCL
    live = slot < counts[dev * N_WIDE + peer]
    picked = coeff_in[src_row].reshape(ndev, blocks, K, R)
    mats = coupling.reshape(ndev, blocks, K, K)

    def one(pair):
        return jnp.einsum("bij,bjr->bir", pair[0].astype(jnp.float32), pair[1].astype(jnp.float32), precision=lax.Precision.HIGHEST)

    partial_value = lax.map(one, (mats, picked)).reshape(ndev * blocks, K * R)
    partial_value = jnp.where(live[:, None], partial_value, jnp.zeros_like(partial_value))
    trow = (grp_i * N_WIDE + peer) * NCL + target
    coeff = jax.ops.segment_sum(partial_value, trow, num_segments=ndev * NCL).reshape(ndev, NCL, K, R)
    trans = transfer.reshape(ndev, NCL - 1, K, K)
    top = coeff[:, 0]
    mid = coeff[:, 1:1 + BRANCH] + jnp.einsum("dcij,djr->dcir", trans[:, :BRANCH], top, precision=lax.Precision.HIGHEST)
    parent = jnp.repeat(mid, BRANCH, axis=1)
    leaves = coeff[:, 1 + BRANCH:] + jnp.einsum("dcij,dcjr->dcir", trans[:, BRANCH:], parent, precision=lax.Precision.HIGHEST)
    bases = basis.reshape(ndev, BRANCH * BRANCH, K, LEAF)
    out = jnp.einsum("dckr,dckp->rdcp", leaves, bases, precision=lax.Precision.HIGHEST)
    return out.reshape(R, NPTS)
```

```python
import functools

import jax
import jax.numpy as jnp
from jax import lax
from jax.experimental import pallas as pl
from jax.experimental.pallas import tpu as pltpu
from jax.sharding import PartitionSpec as P

BRANCH = 8
RANK = 64
RHS = 8
SLOTS = 8
HALF = 4
BF = jnp.bfloat16
F32 = jnp.float32


def split(x):
    high = x.astype(BF)
    low = (x - high.astype(F32)).astype(BF)
    return high, low


def mm(a, b):
    return jnp.dot(a, b, preferred_element_type=F32)


def product3(x, high_ref_value, low_ref_value):
    rows = x.shape[0]
    high, low = split(x)
    both = mm(jnp.concatenate([high, low], axis=0), high_ref_value)
    return both[:rows] + both[rows:] + mm(high, low_ref_value)


def iota(shape, dim):
    return lax.broadcasted_iota(jnp.int32, shape, dim)


def prepare(target, counts, coupling, transfer, basis, ct_h, ct_l, t_h, t_l, b_h, b_l, code):
    nwide = code.shape[0]

    def per_peer(p, carry):
        for s in range(HALF):
            pair = jnp.concatenate([coupling[SLOTS * p + s], coupling[SLOTS * p + HALF + s]], axis=0)
            high, low = split(pair.T)
            ct_h[p, RANK * s : RANK * (s + 1), :] = high
            ct_l[p, RANK * s : RANK * (s + 1), :] = low
        row, lane = iota((8, 128), 0), iota((8, 128), 1)
        value = jnp.zeros((8, 128), jnp.int32)
        for slot in range(SLOTS):
            here = (row == slot // HALF) & ((lane % 32) // RHS == slot % HALF)
            at = jnp.where(slot < counts[p], target[SLOTS * p + slot] * RHS, -RHS)
            value = jnp.where(here, at + lane % RHS, value)
        code[p] = value.astype(F32)
        return carry

    lax.fori_loop(0, nwide, per_peer, 0)
    for g in range(1 + BRANCH):
        block = transfer[BRANCH * g : BRANCH * (g + 1)].reshape(BRANCH * RANK, RANK)
        high, low = split(block.T)
        t_h[RANK * g : RANK * (g + 1), :] = high
        t_l[RANK * g : RANK * (g + 1), :] = low

    def per_group(g, carry):
        rows = pl.ds(pl.multiple_of(g * 256, 256), 256)
        high, low = split(basis[rows, :])
        b_h[rows, :] = high
        b_l[rows, :] = low
        return carry

    lax.fori_loop(0, basis.shape[0] // 256, per_group, 0)


def couple(ntab, idx, *refs):
    tables, (ct_h, ct_l, code, out, held, sems) = refs[:ntab], refs[ntab:]
    nwide = out.shape[0]
    copies = [pltpu.make_async_copy(tables[k], held.at[k], sems.at[k]) for k in range(ntab)]
    for copy in copies:
        copy.start()
    width = RANK * RHS
    gather = jnp.where(iota((width, 256), 0) // RHS == iota((width, 256), 1) % RANK, 1.0, 0.0).astype(BF)
    mine = iota((RHS, width), 0) == iota((RHS, width), 1) % RHS
    diagonal = (iota((64, 256), 0) // RHS) % HALF == iota((64, 256), 1) // RANK
    left = iota((32, 128), 1) < RANK
    for copy in copies:
        copy.wait()
    for p in range(nwide):
        picked = []
        for slot in range(SLOTS):
            at = idx[SLOTS * p + slot]
            row = held[at // 128, pl.ds(at % 128, 1), :]
            picked.append(jnp.where(mine, jnp.broadcast_to(row, (RHS, width)), 0.0))
        high, low = split(jnp.concatenate(picked, axis=0))
        x = mm(jnp.concatenate([high, low], axis=0), gather)
        x = jnp.where(diagonal, x[:64] + x[64:], 0.0)
        z = product3(x, ct_h[p], ct_l[p])
        out[p, :32, :] = jnp.where(left, z[:32], z[32:])
        out[p, 32:, :] = code[p]


def downward(arrived, t_h, t_l, b_h, b_l, out, full):
    nwide = arrived.shape[0]
    ncl = full.shape[0] // RHS
    value = jnp.concatenate([arrived[p, :32, :] for p in range(nwide)], axis=0)
    high, low = split(value)
    weights = jnp.concatenate([high, low], axis=1)
    lane = iota((1, 128), 1)
    codes = []
    for h in range(2):
        parts = []
        for q in range(nwide // 4):
            part = arrived[4 * q, 32 + h : 33 + h, :]
            for e in range(1, 4):
                part = jnp.where(lane // 32 == e, arrived[4 * q + e, 32 + h : 33 + h, :], part)
            parts.append(part)
        codes.append(jnp.concatenate(parts, axis=1).astype(jnp.int32))
    total = full.shape[0]
    step = 80
    for at in range(0, total, step):
        rows = min(step, total - at)
        sums = []
        for h in range(2):
            place = iota((rows, 32 * nwide), 0) + at
            hot = jnp.where(place == codes[h], 1.0, 0.0).astype(BF)
            r = mm(hot, weights)
            sums.append(r[:, :128] + r[:, 128:])
        s = jnp.where(iota((rows, 128), 1) < RANK, sums[0], sums[1])
        full[at : at + rows, :] = s + pltpu.roll(s, RANK, 1)

    first = iota((RHS, 128), 1) < RANK

    def pairs(cluster, count):
        parts = []
        for i in range(0, count, 2):
            a = full[RHS * (cluster + i) : RHS * (cluster + i + 1), :]
            b = full[RHS * (cluster + i + 1) : RHS * (cluster + i + 2), :]
            parts.append(jnp.where(first, a, b))
        return jnp.concatenate(parts, axis=1)

    diagonal = iota((32, 256), 0) // RHS == iota((32, 256), 1) // RANK

    def spread(x):
        return jnp.where(diagonal, jnp.concatenate([x] * 4, axis=0), 0.0)

    top = full[:RHS, :RANK]
    middle = pairs(1, BRANCH) + product3(top, t_h[:RANK, :], t_l[:RANK, :])
    for g in range(2):
        at = slice(RANK + 256 * g, RANK + 256 * (g + 1))
        down = product3(spread(middle[:, 256 * g : 256 * (g + 1)]), t_h[at, :], t_l[at, :])
        for c4 in range(4):
            c = 4 * g + c4
            leaves = pairs(1 + BRANCH + BRANCH * c, BRANCH) + down[RHS * c4 : RHS * (c4 + 1), :]
            for half in range(2):
                j = BRANCH * c + 4 * half
                rows = slice(RANK * j, RANK * (j + 4))
                far = product3(spread(leaves[:, 256 * half : 256 * (half + 1)]), b_h[rows, :], b_l[rows, :])
                for l4 in range(4):
                    out[:, 128 * (j + l4) : 128 * (j + l4 + 1)] = far[RHS * l4 : RHS * (l4 + 1), :]


VMEM = pl.BlockSpec(memory_space=pltpu.VMEM)
SMEM = pl.BlockSpec(memory_space=pltpu.SMEM)
ANY = pl.BlockSpec(memory_space=pl.ANY)


def on_device(coeff_in, coupling, source, target, counts, transfer, basis):
    nwide, ngrp = lax.axis_size("wide"), lax.axis_size("grp")
    nblocks = coupling.shape[0]
    ncl, width = coeff_in.shape
    nleaf, rank, points = basis.shape
    tables = [coeff_in]
    for k in range(1, ngrp):
        tables.append(lax.ppermute(coeff_in, "grp", [(i, (i + k) % ngrp) for i in range(ngrp)]))

    shape = jax.ShapeDtypeStruct
    ct = shape((nwide, 4 * rank, 2 * rank), BF)
    tr = shape(((1 + BRANCH) * rank, BRANCH * rank), BF)
    ba = shape((nleaf * rank, points), BF)
    ct_h, ct_l, t_h, t_l, b_h, b_l, code = pl.pallas_call(
        prepare,
        out_shape=(ct, ct, tr, tr, ba, ba, shape((nwide, 8, 128), F32)),
        in_specs=[SMEM, SMEM, VMEM, VMEM, VMEM],
        out_specs=(VMEM,) * 7,
        compiler_params=pltpu.CompilerParams(vmem_limit_bytes=32 << 20),
        cost_estimate=pl.CostEstimate(flops=0, bytes_accessed=20 << 20, transcendentals=0),
        name="prepare",
    )(target, counts, coupling, transfer, basis.reshape(nleaf * rank, points))

    me = lax.axis_index("grp")
    member, local = source // ncl, source % ncl
    idx = lax.rem(me - member + ngrp, ngrp) * 128 + local
    payload = pl.pallas_call(
        functools.partial(couple, ngrp),
        out_shape=shape((nwide, 40, 128), F32),
        in_specs=[SMEM] + [ANY] * ngrp + [VMEM] * 3,
        out_specs=VMEM,
        scratch_shapes=[pltpu.VMEM((ngrp, ncl, width), F32), pltpu.SemaphoreType.DMA((ngrp,))],
        compiler_params=pltpu.CompilerParams(vmem_limit_bytes=32 << 20),
        name="couple",
    )(idx, *tables, ct_h, ct_l, code)

    arrived = lax.all_to_all(payload, "wide", split_axis=0, concat_axis=0, tiled=True)

    return pl.pallas_call(
        downward,
        out_shape=shape((RHS, nleaf * points), F32),
        in_specs=[VMEM] * 5,
        out_specs=VMEM,
        scratch_shapes=[pltpu.VMEM((ncl * RHS, 128), F32)],
        compiler_params=pltpu.CompilerParams(vmem_limit_bytes=32 << 20),
        name="downward",
    )(arrived, t_h, t_l, b_h, b_l)


def solution(mesh):
    placed = (
        P(("grp", "wide"), None),
        P(("grp", "wide"), None, None),
        P(("grp", "wide")),
        P(("grp", "wide")),
        P(("grp", "wide")),
        P(("grp", "wide"), None, None),
        P(("grp", "wide"), None, None),
    )
    return jax.shard_map(
        on_device, mesh=mesh, in_specs=placed, out_specs=P(None, ("grp", "wide")), check_vma=False
    )
```

```python
import functools

import jax
import jax.numpy as jnp
from jax import lax
from jax.experimental import pallas as pl
from jax.experimental.pallas import tpu as pltpu
from jax.sharding import PartitionSpec as P

BRANCH = 8
RANK = 64
RHS = 8
SLOTS = 8
HALF = 4
BF = jnp.bfloat16
F32 = jnp.float32


def split(x):
    high = x.astype(BF)
    low = (x - high.astype(F32)).astype(BF)
    return high, low


def mm(a, b):
    return jnp.dot(a, b, preferred_element_type=F32)


def product3(x, high_ref_value, low_ref_value):
    rows = x.shape[0]
    high, low = split(x)
    both = mm(jnp.concatenate([high, low], axis=0), high_ref_value)
    return both[:rows] + both[rows:] + mm(high, low_ref_value)


def iota(shape, dim):
    return lax.broadcasted_iota(jnp.int32, shape, dim)


def prepare(target, counts, after, coupling, transfer, ct_h, ct_l, t_h, t_l, code):
    del after
    nwide = code.shape[0]

    def per_peer(p, carry):
        for s in range(HALF):
            pair = jnp.concatenate([coupling[SLOTS * p + s], coupling[SLOTS * p + HALF + s]], axis=0)
            high, low = split(pair.T)
            ct_h[p, RANK * s : RANK * (s + 1), :] = high
            ct_l[p, RANK * s : RANK * (s + 1), :] = low
        row, lane = iota((8, 128), 0), iota((8, 128), 1)
        value = jnp.zeros((8, 128), jnp.int32)
        for slot in range(SLOTS):
            here = (row == slot // HALF) & ((lane % 32) // RHS == slot % HALF)
            at = jnp.where(slot < counts[p], target[SLOTS * p + slot] * RHS, -RHS)
            value = jnp.where(here, at + lane % RHS, value)
        code[p] = value.astype(F32)
        return carry

    lax.fori_loop(0, nwide, per_peer, 0)
    for g in range(1 + BRANCH):
        block = transfer[BRANCH * g : BRANCH * (g + 1)].reshape(BRANCH * RANK, RANK)
        high, low = split(block.T)
        t_h[RANK * g : RANK * (g + 1), :] = high
        t_l[RANK * g : RANK * (g + 1), :] = low


def couple(ntab, idx, *refs):
    tables, (ct_h, ct_l, code, out, held, rows_h, spread_out) = refs[:ntab], refs[ntab:]
    nwide = out.shape[0]
    width = RANK * RHS
    gather = jnp.where(iota((width, 256), 0) // RHS == iota((width, 256), 1) % RANK, 1.0, 0.0).astype(BF)
    mine = iota((RHS, width), 0) == iota((RHS, width), 1) % RHS
    diagonal = (iota((64, 256), 0) // RHS) % HALF == iota((64, 256), 1) // RANK
    left = iota((32, 128), 1) < RANK
    for k in range(ntab):
        held[k] = tables[k][...]
    for p in range(nwide):
        picked = []
        for slot in range(SLOTS):
            at = idx[SLOTS * p + slot]
            row = held[at // 128, pl.ds(at % 128, 1), :]
            picked.append(jnp.where(mine, jnp.broadcast_to(row, (RHS, width)), 0.0))
        high, low = split(jnp.concatenate(picked, axis=0))
        rows_h[128 * p : 128 * p + 64, :] = high
        rows_h[128 * p + 64 : 128 * p + 128, :] = low
    spread_out[...] = mm(rows_h[...], gather)
    for p in range(nwide):
        x = spread_out[128 * p : 128 * p + 64, :] + spread_out[128 * p + 64 : 128 * p + 128, :]
        x = jnp.where(diagonal, x, 0.0)
        z = product3(x, ct_h[p], ct_l[p])
        out[p, :32, :] = jnp.where(left, z[:32], z[32:])
        out[p, 32:, :] = code[p]


def downward(arrived, t_h, t_l, basis, out, full):
    nwide = arrived.shape[0]
    ncl = full.shape[0] // RHS
    value = jnp.concatenate([arrived[p, :32, :] for p in range(nwide)], axis=0)
    high, low = split(value)
    weights = jnp.concatenate([high, low], axis=1)
    lane = iota((1, 128), 1)
    codes = []
    for h in range(2):
        parts = []
        for q in range(nwide // 4):
            part = arrived[4 * q, 32 + h : 33 + h, :]
            for e in range(1, 4):
                part = jnp.where(lane // 32 == e, arrived[4 * q + e, 32 + h : 33 + h, :], part)
            parts.append(part)
        codes.append(jnp.concatenate(parts, axis=1).astype(jnp.int32))
    total = full.shape[0]
    step = 80
    for at in range(0, total, step):
        rows = min(step, total - at)
        sums = []
        for h in range(2):
            place = iota((rows, 32 * nwide), 0) + at
            hot = jnp.where(place == codes[h], 1.0, 0.0).astype(BF)
            r = mm(hot, weights)
            sums.append(r[:, :128] + r[:, 128:])
        s = jnp.where(iota((rows, 128), 1) < RANK, sums[0], sums[1])
        full[at : at + rows, :] = s + pltpu.roll(s, RANK, 1)

    first = iota((RHS, 128), 1) < RANK

    def pairs(cluster, count):
        parts = []
        for i in range(0, count, 2):
            a = full[RHS * (cluster + i) : RHS * (cluster + i + 1), :]
            b = full[RHS * (cluster + i + 1) : RHS * (cluster + i + 2), :]
            parts.append(jnp.where(first, a, b))
        return jnp.concatenate(parts, axis=1)

    diagonal = iota((32, 256), 0) // RHS == iota((32, 256), 1) // RANK

    def spread(x):
        return jnp.where(diagonal, jnp.concatenate([x] * 4, axis=0), 0.0)

    top = full[:RHS, :RANK]
    middle = pairs(1, BRANCH) + product3(top, t_h[:RANK, :], t_l[:RANK, :])
    for g in range(2):
        at = slice(RANK + 256 * g, RANK + 256 * (g + 1))
        down = product3(spread(middle[:, 256 * g : 256 * (g + 1)]), t_h[at, :], t_l[at, :])
        for c4 in range(4):
            c = 4 * g + c4
            leaves = pairs(1 + BRANCH + BRANCH * c, BRANCH) + down[RHS * c4 : RHS * (c4 + 1), :]
            for half in range(2):
                j = BRANCH * c + 4 * half
                rows = slice(RANK * j, RANK * (j + 4))
                far = product3(spread(leaves[:, 256 * half : 256 * (half + 1)]), *split(basis[rows, :]))
                for l4 in range(4):
                    out[:, 128 * (j + l4) : 128 * (j + l4 + 1)] = far[RHS * l4 : RHS * (l4 + 1), :]


VMEM = pl.BlockSpec(memory_space=pltpu.VMEM)
SMEM = pl.BlockSpec(memory_space=pltpu.SMEM)
ANY = pl.BlockSpec(memory_space=pl.ANY)


def gathered(x, n):
    if n != 4:
        rest = [lax.ppermute(x, "grp", [(i, (i + k) % n) for i in range(n)]) for k in range(1, n)]
        return [x] + rest, lambda me, member: lax.rem(me - member + n, n)
    far = lax.ppermute(x, "grp", [(i, 3 - i) for i in range(n)])
    near = lax.ppermute(x, "grp", [(i, i ^ 1) for i in range(n)])
    cross = lax.ppermute(far, "grp", [(i, i ^ 1) for i in range(n)])

    def place(me, member):
        other = jnp.where(member == me ^ 1, 2, 3)
        return jnp.where(member == me, 0, jnp.where(member == 3 - me, 1, other))

    return [x, far, near, cross], place


def on_device(coeff_in, coupling, source, target, counts, transfer, basis):
    nwide, ngrp = lax.axis_size("wide"), lax.axis_size("grp")
    nblocks = coupling.shape[0]
    ncl, width = coeff_in.shape
    nleaf, rank, points = basis.shape
    tables, place = gathered(coeff_in, ngrp)

    shape = jax.ShapeDtypeStruct
    ct = shape((nwide, 4 * rank, 2 * rank), BF)
    tr = shape(((1 + BRANCH) * rank, BRANCH * rank), BF)
    ct_h, ct_l, t_h, t_l, code = pl.pallas_call(
        prepare,
        out_shape=(ct, ct, tr, tr, shape((nwide, 8, 128), F32)),
        in_specs=[SMEM, SMEM, ANY, VMEM, VMEM],
        out_specs=(VMEM,) * 5,
        compiler_params=pltpu.CompilerParams(vmem_limit_bytes=32 << 20),
        cost_estimate=pl.CostEstimate(flops=0, bytes_accessed=20 << 20, transcendentals=0),
        name="prepare",
    )(target, counts, tables[1], coupling, transfer)

    me = lax.axis_index("grp")
    member, local = source // ncl, source % ncl
    idx = place(me, member) * 128 + local
    payload = pl.pallas_call(
        functools.partial(couple, ngrp),
        out_shape=shape((nwide, 40, 128), F32),
        in_specs=[SMEM] + [VMEM] * (ngrp + 3),
        out_specs=VMEM,
        scratch_shapes=[
            pltpu.VMEM((len(tables), ncl, width), F32),
            pltpu.VMEM((2 * nblocks * RHS, width), BF),
            pltpu.VMEM((2 * nblocks * RHS, 256), F32),
        ],
        compiler_params=pltpu.CompilerParams(vmem_limit_bytes=32 << 20),
        name="couple",
    )(idx, *tables, ct_h, ct_l, code)

    arrived = lax.all_to_all(payload, "wide", split_axis=0, concat_axis=0, tiled=True)

    return pl.pallas_call(
        downward,
        out_shape=shape((RHS, nleaf * points), F32),
        in_specs=[VMEM] * 4,
        out_specs=VMEM,
        scratch_shapes=[pltpu.VMEM((ncl * RHS, 128), F32)],
        compiler_params=pltpu.CompilerParams(vmem_limit_bytes=32 << 20),
        name="downward",
    )(arrived, t_h, t_l, basis.reshape(nleaf * rank, points))


def solution(mesh):
    placed = (
        P(("grp", "wide"), None),
        P(("grp", "wide"), None, None),
        P(("grp", "wide")),
        P(("grp", "wide")),
        P(("grp", "wide")),
        P(("grp", "wide"), None, None),
        P(("grp", "wide"), None, None),
    )
    return jax.shard_map(
        on_device, mesh=mesh, in_specs=placed, out_specs=P(None, ("grp", "wide")), check_vma=False
    )
```

```python
import functools

import jax
import jax.numpy as jnp
from jax import lax
from jax.experimental import pallas as pl
from jax.experimental.pallas import tpu as pltpu
from jax.sharding import PartitionSpec as P

BRANCH = 8
RANK = 64
RHS = 8
SLOTS = 8
HALF = 4
BF = jnp.bfloat16
F32 = jnp.float32


def split(x):
    high = x.astype(BF)
    low = (x - high.astype(F32)).astype(BF)
    return high, low


def mm(a, b):
    return jnp.dot(a, b, preferred_element_type=F32)


def product3(x, high_ref_value, low_ref_value):
    rows = x.shape[0]
    high, low = split(x)
    both = mm(jnp.concatenate([high, low], axis=0), high_ref_value)
    return both[:rows] + both[rows:] + mm(high, low_ref_value)


def iota(shape, dim):
    return lax.broadcasted_iota(jnp.int32, shape, dim)


CHUNKS = 4


def prepare(target, counts, coupling_in, transfer_in, ct, t_h, t_l, code, coupling, transfer, turned, sems):
    nwide = code.shape[0]
    ncl = transfer.shape[2]

    def chunks(source, held, at):
        size = held.shape[0] // CHUNKS
        return [
            pltpu.make_async_copy(source.at[pl.ds(size * k, size)], held.at[pl.ds(size * k, size)], sems.at[at + k])
            for k in range(CHUNKS)
        ]

    first, second = chunks(transfer_in, transfer, 0), chunks(coupling_in, coupling, CHUNKS)
    for copy in first + second:
        copy.start()

    def codes(p, carry):
        row, lane = iota((8, 128), 0), iota((8, 128), 1)
        value = jnp.zeros((8, 128), jnp.int32)
        for slot in range(SLOTS):
            here = (row == slot // HALF) & ((lane % 32) // RHS == slot % HALF)
            at = jnp.where(slot < counts[p], target[SLOTS * p + slot] * RHS, -RHS)
            value = jnp.where(here, at + lane % RHS, value)
        code[p] = value.astype(F32)
        return carry

    lax.fori_loop(0, nwide, codes, 0)
    for i in range(RANK):
        if i % (RANK // CHUNKS) == 0:
            first[i // (RANK // CHUNKS)].wait()
        turned[ncl * i : ncl * (i + 1), :] = transfer[i].T
    for g in range(1 + BRANCH):
        rows = [turned[pl.ds(BRANCH * g + c, RANK, stride=ncl), :] for c in range(BRANCH)]
        high, low = split(jnp.concatenate(rows, axis=0).T)
        t_h[RANK * g : RANK * (g + 1), :] = high
        t_l[RANK * g : RANK * (g + 1), :] = low

    def turn(p, carry):
        for s in range(HALF):
            pair = jnp.concatenate([coupling[SLOTS * p + s], coupling[SLOTS * p + HALF + s]], axis=0)
            high, low = split(pair.T)
            ct[p, RANK * s : RANK * (s + 1), :128] = high
            ct[p, RANK * s : RANK * (s + 1), 128:] = low
        return carry

    for k in range(CHUNKS):
        second[k].wait()
        lax.fori_loop(nwide // CHUNKS * k, nwide // CHUNKS * (k + 1), turn, 0, unroll=2)


def pick(two_step, last, source, *refs):
    tables, (early, hot, rows) = refs[:-3], refs[-3:]
    ntab = len(tables) + 1
    ncl = tables[0].shape[0]
    grp = lax.axis_index("grp")
    for k, table in enumerate(tables):
        rows[k] = table[...]
    rows[ntab - 1] = jnp.zeros(rows.shape[1:], F32)
    lane = iota((1, 128), 1)
    marks = []
    for b in range(early.shape[0]):
        at = source[b]
        member = sum(jnp.where(at >= ncl * k, 1, 0) for k in range(1, ntab))
        table = member ^ grp if two_step else lax.rem(grp - member + ntab, ntab)
        held = jnp.where(table == last, ntab - 1, table - jnp.where(table > last, 1, 0))
        local = at - ncl * member
        early[b : b + 1, :] = rows[held, pl.ds(local, 1), :]
        marks.append(jnp.where(lane == jnp.where(table == last, local, -1), 1.0, 0.0))
    hot[...] = jnp.concatenate(marks, axis=0).astype(BF)


def couple(two_step, early, hot, last, ct, code, same, other, held_a, held_b):
    nwide = code.shape[0]
    nblocks, width = early.shape
    ncl = last.shape[0]
    wide = lax.axis_index("wide") if two_step else 0
    high, low = split(jnp.concatenate([last[...], jnp.zeros((128 - ncl, width), F32)], axis=0))
    picked = early[...] + (mm(hot[...], high) + mm(hot[...], low))
    place, to = iota((width, 256), 0), iota((width, 256), 1)
    turn = (place // RHS == to % RANK) & (place % RHS // 2 == to // RANK)
    turn = jnp.where(turn, 1.0, 0.0).astype(BF)
    odd = iota((nblocks, width), 1) % 2
    high, low = split(jnp.concatenate([jnp.where(odd == i, picked, 0.0) for i in range(2)], axis=0))
    turned = mm(jnp.concatenate([high, low], axis=0), turn)
    turned = turned[: 2 * nblocks] + turned[2 * nblocks :]
    first = iota((nblocks, 128), 1) < RANK
    own = iota((nblocks, 128), 0) % HALF - iota((nblocks, 128), 1) // RANK
    for s in range(4):
        for i in range(2):
            x = turned[nblocks * i : nblocks * (i + 1), 128 * (s // 2) : 128 * (s // 2 + 1)]
            swapped = pltpu.roll(x, RANK, 1)
            x = jnp.where(first, x, swapped) if s % 2 == 0 else jnp.where(first, swapped, x)
            rows = pl.ds(2 * s + i, nblocks, stride=RHS)
            held_a[rows, :] = jnp.where(own == 0, x, 0.0)
            held_b[rows, :] = jnp.where(own == 2, x, 0.0)
    left = iota((32, 128), 1) < RANK
    for p in range(nwide):
        peer = p ^ wide
        at = pl.ds(pl.multiple_of(peer * 64, 64), 64)
        high, low = split(jnp.concatenate([held_a[at, :], held_b[at, :]], axis=1))
        z = mm(jnp.concatenate([high, low], axis=0), ct[peer])
        z = z[:64, :128] + (z[:64, 128:] + z[64:, :128])
        out = other if p % 2 else same
        out[p // 2, :32, :] = jnp.where(left, z[:32], z[32:])
        out[p // 2, 32:, :] = code[peer]


def downward(counts, *refs):
    arrays, (t_h, t_l, basis, out, full) = refs[: len(counts)], refs[len(counts) :]
    arrived = [array.at[i] for array, count in zip(arrays, counts) for i in range(count)]
    nwide = len(arrived)
    ncl = full.shape[0] // RHS
    value = jnp.concatenate([arrived[p][:32, :] for p in range(nwide)], axis=0)
    high, low = split(value)
    weights = jnp.concatenate([high, low], axis=1)
    lane = iota((1, 128), 1)
    codes = []
    for h in range(2):
        parts = []
        for q in range(nwide // 4):
            part = arrived[4 * q][32 + h : 33 + h, :]
            for e in range(1, 4):
                part = jnp.where(lane // 32 == e, arrived[4 * q + e][32 + h : 33 + h, :], part)
            parts.append(part)
        codes.append(jnp.concatenate(parts, axis=1).astype(jnp.int32))
    total = full.shape[0]
    step = 80
    for at in range(0, total, step):
        rows = min(step, total - at)
        sums = []
        for h in range(2):
            place = iota((rows, 32 * nwide), 0) + at
            hot = jnp.where(place == codes[h], 1.0, 0.0).astype(BF)
            r = mm(hot, weights)
            sums.append(r[:, :128] + r[:, 128:])
        s = jnp.where(iota((rows, 128), 1) < RANK, sums[0], sums[1])
        full[at : at + rows, :] = s + pltpu.roll(s, RANK, 1)

    first = iota((RHS, 128), 1) < RANK

    def pairs(cluster, count):
        parts = []
        for i in range(0, count, 2):
            a = full[RHS * (cluster + i) : RHS * (cluster + i + 1), :]
            b = full[RHS * (cluster + i + 1) : RHS * (cluster + i + 2), :]
            parts.append(jnp.where(first, a, b))
        return jnp.concatenate(parts, axis=1)

    diagonal = iota((32, 256), 0) // RHS == iota((32, 256), 1) // RANK

    def spread(x):
        return jnp.where(diagonal, jnp.concatenate([x] * 4, axis=0), 0.0)

    top = full[:RHS, :RANK]
    middle = pairs(1, BRANCH) + product3(top, t_h[:RANK, :], t_l[:RANK, :])
    for g in range(2):
        at = slice(RANK + 256 * g, RANK + 256 * (g + 1))
        down = product3(spread(middle[:, 256 * g : 256 * (g + 1)]), t_h[at, :], t_l[at, :])
        for c4 in range(4):
            c = 4 * g + c4
            leaves = pairs(1 + BRANCH + BRANCH * c, BRANCH) + down[RHS * c4 : RHS * (c4 + 1), :]
            for half in range(2):
                j = BRANCH * c + 4 * half
                rows = slice(RANK * j, RANK * (j + 4))
                far = product3(spread(leaves[:, 256 * half : 256 * (half + 1)]), *split(basis[rows, :]))
                for l4 in range(4):
                    out[:, 128 * (j + l4) : 128 * (j + l4 + 1)] = far[RHS * l4 : RHS * (l4 + 1), :]


VMEM = pl.BlockSpec(memory_space=pltpu.VMEM)
SMEM = pl.BlockSpec(memory_space=pltpu.SMEM)
ANY = pl.BlockSpec(memory_space=pl.ANY)


def on_device(coeff_in, coupling, source, target, counts, transfer, basis):
    nwide, ngrp = lax.axis_size("wide"), lax.axis_size("grp")
    nblocks = coupling.shape[0]
    ncl, width = coeff_in.shape
    nleaf, rank, points = basis.shape
    two_step = ngrp == 4 and nwide == 8

    shape = jax.ShapeDtypeStruct
    ct = shape((nwide, 4 * rank, 4 * rank), BF)
    tr = shape(((1 + BRANCH) * rank, BRANCH * rank), BF)
    turned = jnp.transpose(transfer, (1, 2, 0))
    ct, t_h, t_l, code = pl.pallas_call(
        prepare,
        out_shape=(ct, tr, tr, shape((nwide, 8, 128), F32)),
        in_specs=[SMEM, SMEM, ANY, ANY],
        out_specs=(VMEM,) * 4,
        scratch_shapes=[
            pltpu.VMEM(coupling.shape, F32),
            pltpu.VMEM(turned.shape, F32),
            pltpu.VMEM((rank * (ncl - 1), rank), F32),
            pltpu.SemaphoreType.DMA((2 * CHUNKS,)),
        ],
        compiler_params=pltpu.CompilerParams(vmem_limit_bytes=50 << 20),
        cost_estimate=pl.CostEstimate(flops=0, bytes_accessed=10 << 20, transcendentals=0),
        name="prepare",
    )(target, counts, coupling, turned)

    def moved(x, axis, n, to):
        return lax.ppermute(x, axis, [(i, to(i)) for i in range(n)])

    if two_step:
        far = moved(coeff_in, "grp", ngrp, lambda i: i ^ 3)
        near = moved(coeff_in, "grp", ngrp, lambda i: i ^ 1)
        far, code = lax.optimization_barrier((far, code))
        cross = moved(far, "grp", ngrp, lambda i: i ^ 1)
        tables = [coeff_in, near, cross, far]
    else:
        tables = [coeff_in]
        for k in range(1, ngrp):
            tables.append(moved(coeff_in, "grp", ngrp, lambda i: (i + k) % ngrp))

    last = 2 if two_step else ngrp - 1
    early, hot = pl.pallas_call(
        functools.partial(pick, two_step, last),
        out_shape=(shape((nblocks, width), F32), shape((nblocks, 128), BF)),
        in_specs=[SMEM] + [VMEM] * (ngrp - 1),
        out_specs=(VMEM, VMEM),
        scratch_shapes=[pltpu.VMEM((ngrp, ncl, width), F32)],
        compiler_params=pltpu.CompilerParams(vmem_limit_bytes=16 << 20),
        name="pick",
    )(source, *tables[:last], *tables[last + 1 :])

    half = shape((nwide // 2, 40, 128), F32)
    same, other = pl.pallas_call(
        functools.partial(couple, two_step),
        out_shape=(half, half),
        in_specs=[VMEM] * 5,
        out_specs=(VMEM, VMEM),
        scratch_shapes=[pltpu.VMEM((nblocks * RHS, 128), F32)] * 2,
        compiler_params=pltpu.CompilerParams(vmem_limit_bytes=32 << 20),
        name="couple",
    )(early, hot, tables[last], ct, code)

    if two_step:
        mate = moved(other, "wide", nwide, lambda i: i ^ 1)
        arrived = [same[:1], mate[:1]]
        for k in (3, 2, 1):
            arrived.append(moved(jnp.stack([same[k], mate[k]]), "wide", nwide, lambda i: i ^ (2 * k)))
    else:
        payload = jnp.stack([same, other], axis=1).reshape(nwide, 40, 128)
        arrived = [lax.all_to_all(payload, "wide", split_axis=0, concat_axis=0, tiled=True)]

    return pl.pallas_call(
        functools.partial(downward, tuple(a.shape[0] for a in arrived)),
        out_shape=shape((RHS, nleaf * points), F32),
        in_specs=[VMEM] * (len(arrived) + 3),
        out_specs=VMEM,
        scratch_shapes=[pltpu.VMEM((ncl * RHS, 128), F32)],
        compiler_params=pltpu.CompilerParams(vmem_limit_bytes=32 << 20),
        name="downward",
    )(*arrived, t_h, t_l, basis.reshape(nleaf * rank, points))


def solution(mesh):
    placed = (
        P(("grp", "wide"), None),
        P(("grp", "wide"), None, None),
        P(("grp", "wide")),
        P(("grp", "wide")),
        P(("grp", "wide")),
        P(("grp", "wide"), None, None),
        P(("grp", "wide"), None, None),
    )
    return jax.shard_map(
        on_device, mesh=mesh, in_specs=placed, out_specs=P(None, ("grp", "wide")), check_vma=False
    )
```

```python
import functools

import jax
import jax.numpy as jnp
from jax import lax
from jax.experimental import pallas as pl
from jax.experimental.pallas import tpu as pltpu
from jax.sharding import PartitionSpec as P

BRANCH = 8
RANK = 64
RHS = 8
SLOTS = 8
HALF = 4
BF = jnp.bfloat16
F32 = jnp.float32


def split(x):
    high = x.astype(BF)
    low = (x - high.astype(F32)).astype(BF)
    return high, low


def mm(a, b):
    return jnp.dot(a, b, preferred_element_type=F32)


def product3(x, weights):
    rows, columns = x.shape[0], weights.shape[1] // 2
    both = mm(jnp.concatenate(split(x), axis=0), weights)
    return both[:rows, :columns] + (both[:rows, columns:] + both[rows:, :columns])


def iota(shape, dim):
    return lax.broadcasted_iota(jnp.int32, shape, dim)


CHUNKS = 4


def prepare(target, counts, coupling_in, transfer_in, ct, tr, code, coupling, transfer, turned, sems):
    nwide = code.shape[0]
    ncl = transfer.shape[2]

    def chunks(source, held, at):
        size = held.shape[0] // CHUNKS
        return [
            pltpu.make_async_copy(source.at[pl.ds(size * k, size)], held.at[pl.ds(size * k, size)], sems.at[at + k])
            for k in range(CHUNKS)
        ]

    first, second = chunks(transfer_in, transfer, 0), chunks(coupling_in, coupling, CHUNKS)
    for copy in first + second:
        copy.start()

    def codes(p, carry):
        row, lane = iota((8, 128), 0), iota((8, 128), 1)
        value = jnp.zeros((8, 128), jnp.int32)
        for slot in range(SLOTS):
            here = (row == slot // HALF) & ((lane % 32) // RHS == slot % HALF)
            at = jnp.where(slot < counts[p], target[SLOTS * p + slot] * RHS, -RHS)
            value = jnp.where(here, at + lane % RHS, value)
        code[p] = value.astype(F32)
        return carry

    lax.fori_loop(0, nwide, codes, 0)
    for i in range(RANK):
        if i % (RANK // CHUNKS) == 0:
            first[i // (RANK // CHUNKS)].wait()
        turned[ncl * i : ncl * (i + 1), :] = transfer[i].T
    for g in range(1 + BRANCH):
        rows = [turned[pl.ds(BRANCH * g + c, RANK, stride=ncl), :] for c in range(BRANCH)]
        high, low = split(jnp.concatenate(rows, axis=0).T)
        tr[RANK * g : RANK * (g + 1), : BRANCH * RANK] = high
        tr[RANK * g : RANK * (g + 1), BRANCH * RANK :] = low

    def turn(p, carry):
        for s in range(HALF):
            pair = jnp.concatenate([coupling[SLOTS * p + s], coupling[SLOTS * p + HALF + s]], axis=0)
            high, low = split(pair.T)
            ct[p, RANK * s : RANK * (s + 1), :128] = high
            ct[p, RANK * s : RANK * (s + 1), 128:] = low
        return carry

    for k in range(CHUNKS):
        second[k].wait()
        lax.fori_loop(nwide // CHUNKS * k, nwide // CHUNKS * (k + 1), turn, 0, unroll=2)


def pick(two_step, last, source, *refs):
    tables, (early, hot, rows) = refs[:-3], refs[-3:]
    ntab = len(tables) + 1
    ncl = tables[0].shape[0]
    grp = lax.axis_index("grp")
    for k, table in enumerate(tables):
        rows[k] = table[...]
    rows[ntab - 1] = jnp.zeros(rows.shape[1:], F32)
    lane = iota((1, 128), 1)
    marks = []
    for b in range(early.shape[0]):
        at = source[b]
        member = sum(jnp.where(at >= ncl * k, 1, 0) for k in range(1, ntab))
        table = member ^ grp if two_step else lax.rem(grp - member + ntab, ntab)
        held = jnp.where(table == last, ntab - 1, table - jnp.where(table > last, 1, 0))
        local = at - ncl * member
        early[b : b + 1, :] = rows[held, pl.ds(local, 1), :]
        marks.append(jnp.where(lane == jnp.where(table == last, local, -1), 1.0, 0.0))
    hot[...] = jnp.concatenate(marks, axis=0).astype(BF)


def couple(two_step, early, hot, last, ct, code, other, held_a, held_b):
    nblocks, width = early.shape
    ncl = last.shape[0]
    wide = lax.axis_index("wide") if two_step else 0
    high, low = split(jnp.concatenate([last[...], jnp.zeros((128 - ncl, width), F32)], axis=0))
    picked = early[...] + (mm(hot[...], high) + mm(hot[...], low))
    place, to = iota((width, 256), 0), iota((width, 256), 1)
    turn = (place // RHS == to % RANK) & (place % RHS // 2 == to // RANK)
    turn = jnp.where(turn, 1.0, 0.0).astype(BF)
    odd = iota((nblocks, width), 1) % 2
    high, low = split(jnp.concatenate([jnp.where(odd == i, picked, 0.0) for i in range(2)], axis=0))
    turned = mm(jnp.concatenate([high, low], axis=0), turn)
    turned = turned[: 2 * nblocks] + turned[2 * nblocks :]
    first = iota((nblocks, 128), 1) < RANK
    own = iota((nblocks, 128), 0) % HALF - iota((nblocks, 128), 1) // RANK
    for s in range(4):
        for i in range(2):
            x = turned[nblocks * i : nblocks * (i + 1), 128 * (s // 2) : 128 * (s // 2 + 1)]
            swapped = pltpu.roll(x, RANK, 1)
            x = jnp.where(first, x, swapped) if s % 2 == 0 else jnp.where(first, swapped, x)
            rows = pl.ds(2 * s + i, nblocks, stride=RHS)
            held_a[rows, :] = jnp.where(own == 0, x, 0.0)
            held_b[rows, :] = jnp.where(own == 2, x, 0.0)
    towards(1, wide, 2 if two_step else 0, held_a, held_b, ct, code, other)


def couple_more(two_step, held_a, held_b, ct, code, same):
    towards(0, lax.axis_index("wide") if two_step else 0, 0, held_a, held_b, ct, code, same)


def towards(parity, wide, shift, held_a, held_b, ct, code, out):
    left = iota((32, 128), 1) < RANK
    for p in range(out.shape[0]):
        peer = (2 * p + parity) ^ wide
        at = pl.ds(pl.multiple_of(peer * 64, 64), 64)
        z = product3(jnp.concatenate([held_a[at, :], held_b[at, :]], axis=1), ct[peer])
        out[p, :32, :] = jnp.where(left, z[:32], z[32:])
        out[p, 32:, :] = pltpu.roll(code[peer], shift, 0) if shift else code[peer]


def downward(messages, sets, *refs):
    arrived, (tr, basis, out, full, held, sems) = refs[:messages], refs[messages:]
    nwide = messages * sets
    value = jnp.concatenate([message[: 32 * sets, :] for message in arrived], axis=0)
    high, low = split(value)
    weights = jnp.concatenate([high, low], axis=1)
    lane = iota((1, 128), 1)
    codes = []
    for h in range(2):
        parts = []
        for q in range(nwide // 4):
            part = None
            for e in range(4):
                at = 32 * sets + 2 * (e % sets) + h
                row = arrived[(4 * q + e) // sets][at : at + 1, :]
                part = row if part is None else jnp.where(lane // 32 == e, row, part)
            parts.append(part)
        codes.append(jnp.concatenate(parts, axis=1).astype(jnp.int32))
    total = full.shape[0]
    step = 80
    for at in range(0, total, step):
        rows = min(step, total - at)
        sums = []
        for h in range(2):
            place = iota((rows, 32 * nwide), 0) + at
            hot = jnp.where(place == codes[h], 1.0, 0.0).astype(BF)
            r = mm(hot, weights)
            sums.append(r[:, :128] + r[:, 128:])
        s = jnp.where(iota((rows, 128), 1) < RANK, sums[0], sums[1])
        full[at : at + rows, :] = s + pltpu.roll(s, RANK, 1)

    first = iota((RHS, 128), 1) < RANK

    def pairs(cluster, count):
        parts = []
        for i in range(0, count, 2):
            a = full[RHS * (cluster + i) : RHS * (cluster + i + 1), :]
            b = full[RHS * (cluster + i + 1) : RHS * (cluster + i + 2), :]
            parts.append(jnp.where(first, a, b))
        return jnp.concatenate(parts, axis=1)

    diagonal = iota((32, 256), 0) // RHS == iota((32, 256), 1) // RANK

    def spread(x):
        return jnp.where(diagonal, jnp.concatenate([x] * 4, axis=0), 0.0)

    copies = []
    top = full[:RHS, :RANK]
    middle = pairs(1, BRANCH) + product3(top, tr[:RANK, :])
    for g in range(2):
        at = slice(RANK + 256 * g, RANK + 256 * (g + 1))
        down = product3(spread(middle[:, 256 * g : 256 * (g + 1)]), tr[at, :])
        for c4 in range(4):
            c = 4 * g + c4
            leaves = pairs(1 + BRANCH + BRANCH * c, BRANCH) + down[RHS * c4 : RHS * (c4 + 1), :]
            for half in range(2):
                j = BRANCH * c + 4 * half
                rows = slice(RANK * j, RANK * (j + 4))
                far = product3(spread(leaves[:, 256 * half : 256 * (half + 1)]), jnp.concatenate(split(basis[rows, :]), axis=1))
                for l4 in range(4):
                    held[:, 128 * (j + l4) : 128 * (j + l4 + 1)] = far[RHS * l4 : RHS * (l4 + 1), :]
            at = pl.ds(128 * BRANCH * c, 128 * BRANCH)
            copies.append(pltpu.make_async_copy(held.at[:, at], out.at[:, at], sems.at[c]))
            copies[-1].start()
    for copy in copies:
        copy.wait()


VMEM = pl.BlockSpec(memory_space=pltpu.VMEM)
SMEM = pl.BlockSpec(memory_space=pltpu.SMEM)
ANY = pl.BlockSpec(memory_space=pl.ANY)


def on_device(coeff_in, coupling, source, target, counts, transfer, basis):
    nwide, ngrp = lax.axis_size("wide"), lax.axis_size("grp")
    nblocks = coupling.shape[0]
    ncl, width = coeff_in.shape
    nleaf, rank, points = basis.shape
    two_step = ngrp == 4 and nwide == 8

    shape = jax.ShapeDtypeStruct
    ct = shape((nwide, 4 * rank, 4 * rank), BF)
    tr = shape(((1 + BRANCH) * rank, 2 * BRANCH * rank), BF)
    turned = jnp.transpose(transfer, (1, 2, 0))
    ct, tr, code = pl.pallas_call(
        prepare,
        out_shape=(ct, tr, shape((nwide, 8, 128), F32)),
        in_specs=[SMEM, SMEM, ANY, ANY],
        out_specs=(VMEM,) * 3,
        scratch_shapes=[
            pltpu.VMEM(coupling.shape, F32),
            pltpu.VMEM(turned.shape, F32),
            pltpu.VMEM((rank * (ncl - 1), rank), F32),
            pltpu.SemaphoreType.DMA((2 * CHUNKS,)),
        ],
        compiler_params=pltpu.CompilerParams(vmem_limit_bytes=50 << 20),
        cost_estimate=pl.CostEstimate(flops=0, bytes_accessed=10 << 20, transcendentals=0),
        name="prepare",
    )(target, counts, coupling, turned)

    def moved(x, axis, n, to):
        return lax.ppermute(x, axis, [(i, to(i)) for i in range(n)])

    if two_step:
        far = moved(coeff_in, "grp", ngrp, lambda i: i ^ 3)
        near = moved(coeff_in, "grp", ngrp, lambda i: i ^ 1)
        far, code = lax.optimization_barrier((far, code))
        cross = moved(far, "grp", ngrp, lambda i: i ^ 1)
        tables = [coeff_in, near, cross, far]
    else:
        tables = [coeff_in]
        for k in range(1, ngrp):
            tables.append(moved(coeff_in, "grp", ngrp, lambda i: (i + k) % ngrp))

    last = 2 if two_step else ngrp - 1
    early, hot = pl.pallas_call(
        functools.partial(pick, two_step, last),
        out_shape=(shape((nblocks, width), F32), shape((nblocks, 128), BF)),
        in_specs=[SMEM] + [VMEM] * (ngrp - 1),
        out_specs=(VMEM, VMEM),
        scratch_shapes=[pltpu.VMEM((ngrp, ncl, width), F32)],
        compiler_params=pltpu.CompilerParams(vmem_limit_bytes=16 << 20),
        name="pick",
    )(source, *tables[:last], *tables[last + 1 :])

    half = shape((nwide // 2, 40, 128), F32)
    spread = shape((nblocks * RHS, 128), F32)
    other, held_a, held_b = pl.pallas_call(
        functools.partial(couple, two_step),
        out_shape=(half, spread, spread),
        in_specs=[VMEM] * 5,
        out_specs=(VMEM,) * 3,
        compiler_params=pltpu.CompilerParams(vmem_limit_bytes=32 << 20),
        name="couple",
    )(early, hot, tables[last], ct, code)
    same = pl.pallas_call(
        functools.partial(couple_more, two_step),
        out_shape=half,
        in_specs=[VMEM] * 4,
        out_specs=VMEM,
        compiler_params=pltpu.CompilerParams(vmem_limit_bytes=16 << 20),
        cost_estimate=pl.CostEstimate(flops=0, bytes_accessed=4 << 20, transcendentals=0),
        name="couple_more",
    )(held_a, held_b, ct, code)

    if two_step:
        mate = moved(other, "wide", nwide, lambda i: i ^ 1)
        both = jnp.concatenate([same[:, :32], mate[:, :32], same[:, 32:] + mate[:, 32:]], axis=1)
        arrived = [both[0]]
        for k in (1, 2, 3):
            arrived.append(moved(both[k], "wide", nwide, lambda i: i ^ (2 * k)))
        sets = 2
    else:
        payload = jnp.stack([same, other], axis=1).reshape(nwide, 40, 128)
        payload = lax.all_to_all(payload, "wide", split_axis=0, concat_axis=0, tiled=True)
        arrived = [payload[p] for p in range(nwide)]
        sets = 1

    return pl.pallas_call(
        functools.partial(downward, len(arrived), sets),
        out_shape=shape((RHS, nleaf * points), F32),
        in_specs=[VMEM] * (len(arrived) + 2),
        out_specs=ANY,
        scratch_shapes=[
            pltpu.VMEM((ncl * RHS, 128), F32),
            pltpu.VMEM((RHS, nleaf * points), F32),
            pltpu.SemaphoreType.DMA((BRANCH,)),
        ],
        compiler_params=pltpu.CompilerParams(vmem_limit_bytes=32 << 20),
        name="downward",
    )(*arrived, tr, basis.reshape(nleaf * rank, points))


def solution(mesh):
    placed = (
        P(("grp", "wide"), None),
        P(("grp", "wide"), None, None),
        P(("grp", "wide")),
        P(("grp", "wide")),
        P(("grp", "wide")),
        P(("grp", "wide"), None, None),
        P(("grp", "wide"), None, None),
    )
    return jax.shard_map(
        on_device, mesh=mesh, in_specs=placed, out_specs=P(None, ("grp", "wide")), check_vma=False
    )
```

```python
import functools

import jax
import jax.numpy as jnp
from jax import lax
from jax.experimental import pallas as pl
from jax.experimental.pallas import tpu as pltpu
from jax.sharding import PartitionSpec as P

BRANCH = 8
RANK = 64
RHS = 8
SLOTS = 8
HALF = 4
BF = jnp.bfloat16
F32 = jnp.float32


def split(x):
    high = x.astype(BF)
    low = (x - high.astype(F32)).astype(BF)
    return high, low


def mm(a, b):
    return jnp.dot(a, b, preferred_element_type=F32)


def product3(x, weights):
    rows, columns = x.shape[0], weights.shape[1] // 2
    both = mm(jnp.concatenate(split(x), axis=0), weights)
    return both[:rows, :columns] + (both[:rows, columns:] + both[rows:, :columns])


def iota(shape, dim):
    return lax.broadcasted_iota(jnp.int32, shape, dim)


CHUNKS = 4


def prepare(coupling_in, transfer_in, ct, tr, coupling, transfer, turned, sems):
    nwide = ct.shape[0]
    ncl = transfer.shape[2]

    def chunks(source, held, at):
        size = held.shape[0] // CHUNKS
        return [
            pltpu.make_async_copy(source.at[pl.ds(size * k, size)], held.at[pl.ds(size * k, size)], sems.at[at + k])
            for k in range(CHUNKS)
        ]

    first, second = chunks(transfer_in, transfer, 0), chunks(coupling_in, coupling, CHUNKS)
    for copy in first + second:
        copy.start()

    for i in range(RANK):
        if i % (RANK // CHUNKS) == 0:
            first[i // (RANK // CHUNKS)].wait()
        turned[ncl * i : ncl * (i + 1), :] = transfer[i].T
    for g in range(1 + BRANCH):
        rows = [turned[pl.ds(BRANCH * g + c, RANK, stride=ncl), :] for c in range(BRANCH)]
        high, low = split(jnp.concatenate(rows, axis=0).T)
        tr[RANK * g : RANK * (g + 1), : BRANCH * RANK] = high
        tr[RANK * g : RANK * (g + 1), BRANCH * RANK :] = low

    def turn(p, carry):
        for s in range(HALF):
            pair = jnp.concatenate([coupling[SLOTS * p + s], coupling[SLOTS * p + HALF + s]], axis=0)
            high, low = split(pair.T)
            ct[p, RANK * s : RANK * (s + 1), :128] = high
            ct[p, RANK * s : RANK * (s + 1), 128:] = low
        return carry

    for k in range(CHUNKS):
        second[k].wait()
        lax.fori_loop(nwide // CHUNKS * k, nwide // CHUNKS * (k + 1), turn, 0, unroll=2)


def pick(two_step, source, target, counts, *refs):
    tables, (early, code, rows) = refs[:-3], refs[-3:]
    nmember, ncl = rows.shape[:2]
    nmember = nmember + 1 if two_step else nmember
    grp = lax.axis_index("grp")
    for k, table in enumerate(tables):
        rows[k] = table[...]
    if two_step:
        rows[2] = jnp.zeros(rows.shape[1:], F32)
    for b in range(early.shape[0]):
        at = source[b]
        member = sum(jnp.where(at >= ncl * k, 1, 0) for k in range(1, nmember))
        if two_step:
            apart = member ^ grp
            table = jnp.where(apart == 0, 0, jnp.where(apart == 3, 1, 2))
        else:
            table = lax.rem(grp - member + nmember, nmember)
        early[b : b + 1, :] = rows[table, pl.ds(at - ncl * member, 1), :]
    row, lane = iota((8, 128), 0), iota((8, 128), 1)
    for p in range(code.shape[0]):
        value = jnp.zeros((8, 128), jnp.int32)
        for slot in range(SLOTS):
            here = (row == slot // HALF) & ((lane % 32) // RHS == slot % HALF)
            at = jnp.where(slot < counts[p], target[SLOTS * p + slot] * RHS, -RHS)
            value = jnp.where(here, at + lane % RHS, value)
        code[p] = value.astype(F32)


def relay(theirs, own, far, out):
    ncl, width = own.shape
    grp = lax.axis_index("grp")
    row = iota((128, theirs.shape[1]), 0)
    hot = jnp.concatenate([theirs[...] - ncl * grp == row, theirs[...] - ncl * (grp ^ 3) == row], axis=0)
    hot = jnp.where(hot, 1.0, 0.0).T.astype(BF)
    none = jnp.zeros((128 - ncl, width), F32)
    high, low = split(jnp.concatenate([own[...], none, far[...], none], axis=0))
    out[...] = mm(hot, high) + mm(hot, low)


def couple(two_step, parts, *refs):
    early, (ct, code, other, held_a, held_b) = refs[:parts], refs[parts:]
    nblocks, width = early[0].shape
    wide = lax.axis_index("wide") if two_step else 0
    picked = sum(part[...] for part in early)
    place, to = iota((width, 256), 0), iota((width, 256), 1)
    turn = (place // RHS == to % RANK) & (place % RHS // 2 == to // RANK)
    turn = jnp.where(turn, 1.0, 0.0).astype(BF)
    odd = iota((nblocks, width), 1) % 2
    high, low = split(jnp.concatenate([jnp.where(odd == i, picked, 0.0) for i in range(2)], axis=0))
    turned = mm(jnp.concatenate([high, low], axis=0), turn)
    turned = turned[: 2 * nblocks] + turned[2 * nblocks :]
    first = iota((nblocks, 128), 1) < RANK
    own = iota((nblocks, 128), 0) % HALF - iota((nblocks, 128), 1) // RANK
    for s in range(4):
        for i in range(2):
            x = turned[nblocks * i : nblocks * (i + 1), 128 * (s // 2) : 128 * (s // 2 + 1)]
            swapped = pltpu.roll(x, RANK, 1)
            x = jnp.where(first, x, swapped) if s % 2 == 0 else jnp.where(first, swapped, x)
            rows = pl.ds(2 * s + i, nblocks, stride=RHS)
            held_a[rows, :] = jnp.where(own == 0, x, 0.0)
            held_b[rows, :] = jnp.where(own == 2, x, 0.0)
    towards(1, wide, 2 if two_step else 0, held_a, held_b, ct, code, other)


def couple_more(two_step, held_a, held_b, ct, code, same):
    towards(0, lax.axis_index("wide") if two_step else 0, 0, held_a, held_b, ct, code, same)


def towards(parity, wide, shift, held_a, held_b, ct, code, out):
    left = iota((32, 128), 1) < RANK
    for p in range(out.shape[0]):
        peer = (2 * p + parity) ^ wide
        at = pl.ds(pl.multiple_of(peer * 64, 64), 64)
        z = product3(jnp.concatenate([held_a[at, :], held_b[at, :]], axis=1), ct[peer])
        out[p, :32, :] = jnp.where(left, z[:32], z[32:])
        out[p, 32:, :] = pltpu.roll(code[peer], shift, 0) if shift else code[peer]


def downward(messages, sets, *refs):
    arrived, (tr, basis, out, full, held, sems) = refs[:messages], refs[messages:]
    nwide = messages * sets
    value = jnp.concatenate([message[: 32 * sets, :] for message in arrived], axis=0)
    high, low = split(value)
    weights = jnp.concatenate([high, low], axis=1)
    lane = iota((1, 128), 1)
    codes = []
    for h in range(2):
        parts = []
        for q in range(nwide // 4):
            part = None
            for e in range(4):
                at = 32 * sets + 2 * (e % sets) + h
                row = arrived[(4 * q + e) // sets][at : at + 1, :]
                part = row if part is None else jnp.where(lane // 32 == e, row, part)
            parts.append(part)
        codes.append(jnp.concatenate(parts, axis=1).astype(jnp.int32))
    total = full.shape[0]
    step = 80
    for at in range(0, total, step):
        rows = min(step, total - at)
        sums = []
        for h in range(2):
            place = iota((rows, 32 * nwide), 0) + at
            hot = jnp.where(place == codes[h], 1.0, 0.0).astype(BF)
            r = mm(hot, weights)
            sums.append(r[:, :128] + r[:, 128:])
        s = jnp.where(iota((rows, 128), 1) < RANK, sums[0], sums[1])
        full[at : at + rows, :] = s + pltpu.roll(s, RANK, 1)

    first = iota((RHS, 128), 1) < RANK

    def pairs(cluster, count):
        parts = []
        for i in range(0, count, 2):
            a = full[RHS * (cluster + i) : RHS * (cluster + i + 1), :]
            b = full[RHS * (cluster + i + 1) : RHS * (cluster + i + 2), :]
            parts.append(jnp.where(first, a, b))
        return jnp.concatenate(parts, axis=1)

    diagonal = iota((32, 256), 0) // RHS == iota((32, 256), 1) // RANK

    def spread(x):
        return jnp.where(diagonal, jnp.concatenate([x] * 4, axis=0), 0.0)

    copies = []
    top = full[:RHS, :RANK]
    middle = pairs(1, BRANCH) + product3(top, tr[:RANK, :])
    for g in range(2):
        at = slice(RANK + 256 * g, RANK + 256 * (g + 1))
        down = product3(spread(middle[:, 256 * g : 256 * (g + 1)]), tr[at, :])
        for c4 in range(4):
            c = 4 * g + c4
            leaves = pairs(1 + BRANCH + BRANCH * c, BRANCH) + down[RHS * c4 : RHS * (c4 + 1), :]
            for half in range(2):
                j = BRANCH * c + 4 * half
                rows = slice(RANK * j, RANK * (j + 4))
                far = product3(spread(leaves[:, 256 * half : 256 * (half + 1)]), jnp.concatenate(split(basis[rows, :]), axis=1))
                for l4 in range(4):
                    held[:, 128 * (j + l4) : 128 * (j + l4 + 1)] = far[RHS * l4 : RHS * (l4 + 1), :]
            at = pl.ds(128 * BRANCH * c, 128 * BRANCH)
            copies.append(pltpu.make_async_copy(held.at[:, at], out.at[:, at], sems.at[c]))
            copies[-1].start()
    for copy in copies:
        copy.wait()


VMEM = pl.BlockSpec(memory_space=pltpu.VMEM)
SMEM = pl.BlockSpec(memory_space=pltpu.SMEM)
ANY = pl.BlockSpec(memory_space=pl.ANY)


def on_device(coeff_in, coupling, source, target, counts, transfer, basis):
    nwide, ngrp = lax.axis_size("wide"), lax.axis_size("grp")
    nblocks = coupling.shape[0]
    ncl, width = coeff_in.shape
    nleaf, rank, points = basis.shape
    two_step = ngrp == 4 and nwide == 8

    shape = jax.ShapeDtypeStruct
    ct = shape((nwide, 4 * rank, 4 * rank), BF)
    tr = shape(((1 + BRANCH) * rank, 2 * BRANCH * rank), BF)
    turned = jnp.transpose(transfer, (1, 2, 0))
    ct, tr = pl.pallas_call(
        prepare,
        out_shape=(ct, tr),
        in_specs=[ANY, ANY],
        out_specs=(VMEM,) * 2,
        scratch_shapes=[
            pltpu.VMEM(coupling.shape, F32),
            pltpu.VMEM(turned.shape, F32),
            pltpu.VMEM((rank * (ncl - 1), rank), F32),
            pltpu.SemaphoreType.DMA((2 * CHUNKS,)),
        ],
        compiler_params=pltpu.CompilerParams(vmem_limit_bytes=50 << 20),
        cost_estimate=pl.CostEstimate(flops=0, bytes_accessed=10 << 20, transcendentals=0),
        name="prepare",
    )(coupling, turned)

    def moved(x, axis, n, to):
        return lax.ppermute(x, axis, [(i, to(i)) for i in range(n)])

    if two_step:
        far = moved(coeff_in, "grp", ngrp, lambda i: i ^ 3)
        theirs = moved(source, "grp", ngrp, lambda i: i ^ 1)
        far, theirs = lax.optimization_barrier((far, theirs))
        far, ct = lax.optimization_barrier((far, ct))
        across = pl.pallas_call(
            relay,
            out_shape=shape((nblocks, width), F32),
            in_specs=[VMEM] * 3,
            out_specs=VMEM,
            compiler_params=pltpu.CompilerParams(vmem_limit_bytes=16 << 20),
            name="relay",
        )(theirs.reshape(1, nblocks), coeff_in, far)
        across = moved(across, "grp", ngrp, lambda i: i ^ 1)
        tables = [coeff_in, far]
    else:
        tables = [coeff_in]
        for k in range(1, ngrp):
            tables.append(moved(coeff_in, "grp", ngrp, lambda i: (i + k) % ngrp))

    held = (3 if two_step else ngrp, ncl, width)
    early, code = pl.pallas_call(
        functools.partial(pick, two_step),
        out_shape=(shape((nblocks, width), F32), shape((nwide, 8, 128), F32)),
        in_specs=[SMEM] * 3 + [VMEM] * len(tables),
        out_specs=(VMEM,) * 2,
        scratch_shapes=[pltpu.VMEM(held, F32)],
        compiler_params=pltpu.CompilerParams(vmem_limit_bytes=16 << 20),
        name="pick",
    )(source, target, counts, *tables)
    picked = [early, across] if two_step else [early]

    half = shape((nwide // 2, 40, 128), F32)
    spread = shape((nblocks * RHS, 128), F32)
    other, held_a, held_b = pl.pallas_call(
        functools.partial(couple, two_step, len(picked)),
        out_shape=(half, spread, spread),
        in_specs=[VMEM] * (len(picked) + 2),
        out_specs=(VMEM,) * 3,
        compiler_params=pltpu.CompilerParams(vmem_limit_bytes=32 << 20),
        name="couple",
    )(*picked, ct, code)
    same = pl.pallas_call(
        functools.partial(couple_more, two_step),
        out_shape=half,
        in_specs=[VMEM] * 4,
        out_specs=VMEM,
        compiler_params=pltpu.CompilerParams(vmem_limit_bytes=16 << 20),
        cost_estimate=pl.CostEstimate(flops=0, bytes_accessed=4 << 20, transcendentals=0),
        name="couple_more",
    )(held_a, held_b, ct, code)

    if two_step:
        mate = moved(other, "wide", nwide, lambda i: i ^ 1)
        both = jnp.concatenate([same[:, :32], mate[:, :32], same[:, 32:] + mate[:, 32:]], axis=1)
        arrived = [both[0]]
        for k in (1, 2, 3):
            arrived.append(moved(both[k], "wide", nwide, lambda i: i ^ (2 * k)))
        sets = 2
    else:
        payload = jnp.stack([same, other], axis=1).reshape(nwide, 40, 128)
        payload = lax.all_to_all(payload, "wide", split_axis=0, concat_axis=0, tiled=True)
        arrived = [payload[p] for p in range(nwide)]
        sets = 1

    return pl.pallas_call(
        functools.partial(downward, len(arrived), sets),
        out_shape=shape((RHS, nleaf * points), F32),
        in_specs=[VMEM] * (len(arrived) + 2),
        out_specs=ANY,
        scratch_shapes=[
            pltpu.VMEM((ncl * RHS, 128), F32),
            pltpu.VMEM((RHS, nleaf * points), F32),
            pltpu.SemaphoreType.DMA((BRANCH,)),
        ],
        compiler_params=pltpu.CompilerParams(vmem_limit_bytes=32 << 20),
        name="downward",
    )(*arrived, tr, basis.reshape(nleaf * rank, points))


def solution(mesh):
    placed = (
        P(("grp", "wide"), None),
        P(("grp", "wide"), None, None),
        P(("grp", "wide")),
        P(("grp", "wide")),
        P(("grp", "wide")),
        P(("grp", "wide"), None, None),
        P(("grp", "wide"), None, None),
    )
    return jax.shard_map(
        on_device, mesh=mesh, in_specs=placed, out_specs=P(None, ("grp", "wide")), check_vma=False
    )
```

```python
import functools

import jax
import jax.numpy as jnp
from jax import lax
from jax.experimental import pallas as pl
from jax.experimental.pallas import tpu as pltpu
from jax.sharding import PartitionSpec as P

BRANCH = 8
RANK = 64
RHS = 8
SLOTS = 8
HALF = 4
BF = jnp.bfloat16
F32 = jnp.float32


def split(x):
    high = x.astype(BF)
    low = (x - high.astype(F32)).astype(BF)
    return high, low


def mm(a, b):
    return jnp.dot(a, b, preferred_element_type=F32)


def product3(x, weights):
    rows, columns = x.shape[0], weights.shape[1] // 2
    both = mm(jnp.concatenate(split(x), axis=0), weights)
    return both[:rows, :columns] + (both[:rows, columns:] + both[rows:, :columns])


def iota(shape, dim):
    return lax.broadcasted_iota(jnp.int32, shape, dim)


CHUNKS = 4


def prepare(coupling_in, transfer_in, ct, tr, coupling, transfer, turned, sems):
    nwide = ct.shape[0]
    ncl = transfer.shape[2]

    def chunks(source, held, at):
        size = held.shape[0] // CHUNKS
        return [
            pltpu.make_async_copy(source.at[pl.ds(size * k, size)], held.at[pl.ds(size * k, size)], sems.at[at + k])
            for k in range(CHUNKS)
        ]

    first, second = chunks(transfer_in, transfer, 0), chunks(coupling_in, coupling, CHUNKS)
    for copy in first + second:
        copy.start()

    for i in range(RANK):
        if i % (RANK // CHUNKS) == 0:
            first[i // (RANK // CHUNKS)].wait()
        turned[ncl * i : ncl * (i + 1), :] = transfer[i].T
    for g in range(1 + BRANCH):
        rows = [turned[pl.ds(BRANCH * g + c, RANK, stride=ncl), :] for c in range(BRANCH)]
        high, low = split(jnp.concatenate(rows, axis=0).T)
        tr[RANK * g : RANK * (g + 1), : BRANCH * RANK] = high
        tr[RANK * g : RANK * (g + 1), BRANCH * RANK :] = low

    def turn(p, carry):
        for s in range(HALF):
            pair = jnp.concatenate([coupling[SLOTS * p + s], coupling[SLOTS * p + HALF + s]], axis=0)
            high, low = split(pair.T)
            ct[p, RANK * s : RANK * (s + 1), :128] = high
            ct[p, RANK * s : RANK * (s + 1), 128:] = low
        return carry

    for k in range(CHUNKS):
        second[k].wait()
        lax.fori_loop(nwide // CHUNKS * k, nwide // CHUNKS * (k + 1), turn, 0, unroll=2)


def pick(two_step, source, target, counts, *refs):
    tables, (early, code, rows) = refs[:-3], refs[-3:]
    nmember, ncl = rows.shape[:2]
    nmember = nmember + 1 if two_step else nmember
    grp = lax.axis_index("grp")
    for k, table in enumerate(tables):
        rows[k] = table[...]
    if two_step:
        rows[2] = jnp.zeros(rows.shape[1:], F32)
    for b in range(early.shape[0]):
        at = source[b]
        member = sum(jnp.where(at >= ncl * k, 1, 0) for k in range(1, nmember))
        if two_step:
            apart = member ^ grp
            table = jnp.where(apart == 0, 0, jnp.where(apart == 3, 1, 2))
        else:
            table = lax.rem(grp - member + nmember, nmember)
        early[b : b + 1, :] = rows[table, pl.ds(at - ncl * member, 1), :]
    row, lane = iota((8, 128), 0), iota((8, 128), 1)
    for p in range(code.shape[0]):
        value = jnp.zeros((8, 128), jnp.int32)
        for slot in range(SLOTS):
            here = (row == slot // HALF) & ((lane % 32) // RHS == slot % HALF)
            at = jnp.where(slot < counts[p], target[SLOTS * p + slot] * RHS, -RHS)
            value = jnp.where(here, at + lane % RHS, value)
        code[p] = value.astype(F32)


def relay(theirs, own, far, out):
    ncl, width = own.shape
    grp = lax.axis_index("grp")
    row = iota((128, theirs.shape[1]), 0)
    hot = jnp.concatenate([theirs[...] - ncl * grp == row, theirs[...] - ncl * (grp ^ 3) == row], axis=0)
    hot = jnp.where(hot, 1.0, 0.0).T.astype(BF)
    none = jnp.zeros((128 - ncl, width), F32)
    high, low = split(jnp.concatenate([own[...], none, far[...], none], axis=0))
    out[...] = mm(hot, high) + mm(hot, low)


def couple(two_step, parts, *refs):
    early, (ct, code, other, held_a, held_b) = refs[:parts], refs[parts:]
    nblocks, width = early[0].shape
    wide = lax.axis_index("wide") if two_step else 0
    picked = sum(part[...] for part in early)
    place, to = iota((width, 256), 0), iota((width, 256), 1)
    turn = (place // RHS == to % RANK) & (place % RHS // 2 == to // RANK)
    turn = jnp.where(turn, 1.0, 0.0).astype(BF)
    odd = iota((nblocks, width), 1) % 2
    high, low = split(jnp.concatenate([jnp.where(odd == i, picked, 0.0) for i in range(2)], axis=0))
    turned = mm(jnp.concatenate([high, low], axis=0), turn)
    turned = turned[: 2 * nblocks] + turned[2 * nblocks :]
    first = iota((nblocks, 128), 1) < RANK
    own = iota((nblocks, 128), 0) % HALF - iota((nblocks, 128), 1) // RANK
    for s in range(4):
        for i in range(2):
            x = turned[nblocks * i : nblocks * (i + 1), 128 * (s // 2) : 128 * (s // 2 + 1)]
            swapped = pltpu.roll(x, RANK, 1)
            x = jnp.where(first, x, swapped) if s % 2 == 0 else jnp.where(first, swapped, x)
            rows = pl.ds(2 * s + i, nblocks, stride=RHS)
            held_a[rows, :] = jnp.where(own == 0, x, 0.0)
            held_b[rows, :] = jnp.where(own == 2, x, 0.0)
    towards(1, wide, 2 if two_step else 0, held_a, held_b, ct, code, other)


def couple_more(two_step, held_a, held_b, ct, code, same):
    towards(0, lax.axis_index("wide") if two_step else 0, 0, held_a, held_b, ct, code, same)


def towards(parity, wide, shift, held_a, held_b, ct, code, out):
    left = iota((32, 128), 1) < RANK
    for p in range(out.shape[0]):
        peer = (2 * p + parity) ^ wide
        at = pl.ds(pl.multiple_of(peer * 64, 64), 64)
        z = product3(jnp.concatenate([held_a[at, :], held_b[at, :]], axis=1), ct[peer])
        out[p, :32, :] = jnp.where(left, z[:32], z[32:])
        out[p, 32:, :] = pltpu.roll(code[peer], shift, 0) if shift else code[peer]


def downward(messages, sets, *refs):
    arrived, (tr, basis, out, full, held, sems) = refs[:messages], refs[messages:]
    nwide = messages * sets
    value = jnp.concatenate([message[: 32 * sets, :] for message in arrived], axis=0)
    high, low = split(value)
    weights = jnp.concatenate([high, low], axis=1)
    lane = iota((1, 128), 1)
    codes = []
    for h in range(2):
        parts = []
        for q in range(nwide // 4):
            part = None
            for e in range(4):
                at = 32 * sets + 2 * (e % sets) + h
                row = arrived[(4 * q + e) // sets][at : at + 1, :]
                part = row if part is None else jnp.where(lane // 32 == e, row, part)
            parts.append(part)
        codes.append(jnp.concatenate(parts, axis=1).astype(jnp.int32))
    rows = full.shape[0]
    place = iota((rows, 32 * nwide), 0)
    sums = []
    for h in range(2):
        r = mm(jnp.where(place == codes[h], 1.0, 0.0).astype(BF), weights)
        sums.append(r[:, :128] + r[:, 128:])
    s = jnp.where(iota((rows, 128), 1) < RANK, sums[0], sums[1])
    full[...] = s + pltpu.roll(s, RANK, 1)

    first = iota((RHS, 128), 1) < RANK

    def pairs(cluster, count):
        parts = []
        for i in range(0, count, 2):
            a = full[RHS * (cluster + i) : RHS * (cluster + i + 1), :]
            b = full[RHS * (cluster + i + 1) : RHS * (cluster + i + 2), :]
            parts.append(jnp.where(first, a, b))
        return jnp.concatenate(parts, axis=1)

    diagonal = iota((32, 256), 0) // RHS == iota((32, 256), 1) // RANK

    def spread(x):
        return jnp.where(diagonal, jnp.concatenate([x] * 4, axis=0), 0.0)

    copies = []
    top = full[:RHS, :RANK]
    middle = pairs(1, BRANCH) + product3(top, tr[:RANK, :])
    for g in range(2):
        at = slice(RANK + 256 * g, RANK + 256 * (g + 1))
        down = product3(spread(middle[:, 256 * g : 256 * (g + 1)]), tr[at, :])
        for c4 in range(4):
            c = 4 * g + c4
            leaves = pairs(1 + BRANCH + BRANCH * c, BRANCH) + down[RHS * c4 : RHS * (c4 + 1), :]
            for half in range(2):
                j = BRANCH * c + 4 * half
                rows = slice(RANK * j, RANK * (j + 4))
                far = product3(spread(leaves[:, 256 * half : 256 * (half + 1)]), jnp.concatenate(split(basis[rows, :]), axis=1))
                for l4 in range(4):
                    held[:, 128 * (j + l4) : 128 * (j + l4 + 1)] = far[RHS * l4 : RHS * (l4 + 1), :]
            at = pl.ds(128 * BRANCH * c, 128 * BRANCH)
            copies.append(pltpu.make_async_copy(held.at[:, at], out.at[:, at], sems.at[c]))
            copies[-1].start()
    for copy in copies:
        copy.wait()


VMEM = pl.BlockSpec(memory_space=pltpu.VMEM)
SMEM = pl.BlockSpec(memory_space=pltpu.SMEM)
ANY = pl.BlockSpec(memory_space=pl.ANY)


def on_device(coeff_in, coupling, source, target, counts, transfer, basis):
    nwide, ngrp = lax.axis_size("wide"), lax.axis_size("grp")
    nblocks = coupling.shape[0]
    ncl, width = coeff_in.shape
    nleaf, rank, points = basis.shape
    two_step = ngrp == 4 and nwide == 8

    shape = jax.ShapeDtypeStruct
    ct = shape((nwide, 4 * rank, 4 * rank), BF)
    tr = shape(((1 + BRANCH) * rank, 2 * BRANCH * rank), BF)
    turned = jnp.transpose(transfer, (1, 2, 0))
    ct, tr = pl.pallas_call(
        prepare,
        out_shape=(ct, tr),
        in_specs=[ANY, ANY],
        out_specs=(VMEM,) * 2,
        scratch_shapes=[
            pltpu.VMEM(coupling.shape, F32),
            pltpu.VMEM(turned.shape, F32),
            pltpu.VMEM((rank * (ncl - 1), rank), F32),
            pltpu.SemaphoreType.DMA((2 * CHUNKS,)),
        ],
        compiler_params=pltpu.CompilerParams(vmem_limit_bytes=50 << 20),
        cost_estimate=pl.CostEstimate(flops=0, bytes_accessed=10 << 20, transcendentals=0),
        name="prepare",
    )(coupling, turned)

    def moved(x, axis, n, to):
        return lax.ppermute(x, axis, [(i, to(i)) for i in range(n)])

    if two_step:
        far = moved(coeff_in, "grp", ngrp, lambda i: i ^ 3)
        theirs = moved(source, "grp", ngrp, lambda i: i ^ 1)
        far, theirs = lax.optimization_barrier((far, theirs))
        far, ct = lax.optimization_barrier((far, ct))
        across = pl.pallas_call(
            relay,
            out_shape=shape((nblocks, width), F32),
            in_specs=[VMEM] * 3,
            out_specs=VMEM,
            compiler_params=pltpu.CompilerParams(vmem_limit_bytes=16 << 20),
            name="relay",
        )(theirs.reshape(1, nblocks), coeff_in, far)
        across = moved(across, "grp", ngrp, lambda i: i ^ 1)
        tables = [coeff_in, far]
    else:
        tables = [coeff_in]
        for k in range(1, ngrp):
            tables.append(moved(coeff_in, "grp", ngrp, lambda i: (i + k) % ngrp))

    held = (3 if two_step else ngrp, ncl, width)
    early, code = pl.pallas_call(
        functools.partial(pick, two_step),
        out_shape=(shape((nblocks, width), F32), shape((nwide, 8, 128), F32)),
        in_specs=[SMEM] * 3 + [VMEM] * len(tables),
        out_specs=(VMEM,) * 2,
        scratch_shapes=[pltpu.VMEM(held, F32)],
        compiler_params=pltpu.CompilerParams(vmem_limit_bytes=16 << 20),
        name="pick",
    )(source, target, counts, *tables)
    picked = [early, across] if two_step else [early]

    half = shape((nwide // 2, 40, 128), F32)
    spread = shape((nblocks * RHS, 128), F32)
    other, held_a, held_b = pl.pallas_call(
        functools.partial(couple, two_step, len(picked)),
        out_shape=(half, spread, spread),
        in_specs=[VMEM] * (len(picked) + 2),
        out_specs=(VMEM,) * 3,
        compiler_params=pltpu.CompilerParams(vmem_limit_bytes=32 << 20),
        name="couple",
    )(*picked, ct, code)
    same = pl.pallas_call(
        functools.partial(couple_more, two_step),
        out_shape=half,
        in_specs=[VMEM] * 4,
        out_specs=VMEM,
        compiler_params=pltpu.CompilerParams(vmem_limit_bytes=16 << 20),
        cost_estimate=pl.CostEstimate(flops=0, bytes_accessed=4 << 20, transcendentals=0),
        name="couple_more",
    )(held_a, held_b, ct, code)

    if two_step:
        mate = moved(other, "wide", nwide, lambda i: i ^ 1)
        both = jnp.concatenate([same[:, :32], mate[:, :32], same[:, 32:] + mate[:, 32:]], axis=1)
        arrived = [both[0]]
        for k in (1, 2, 3):
            arrived.append(moved(both[k], "wide", nwide, lambda i: i ^ (2 * k)))
        sets = 2
    else:
        payload = jnp.stack([same, other], axis=1).reshape(nwide, 40, 128)
        payload = lax.all_to_all(payload, "wide", split_axis=0, concat_axis=0, tiled=True)
        arrived = [payload[p] for p in range(nwide)]
        sets = 1

    return pl.pallas_call(
        functools.partial(downward, len(arrived), sets),
        out_shape=shape((RHS, nleaf * points), F32),
        in_specs=[VMEM] * (len(arrived) + 2),
        out_specs=ANY,
        scratch_shapes=[
            pltpu.VMEM((ncl * RHS, 128), F32),
            pltpu.VMEM((RHS, nleaf * points), F32),
            pltpu.SemaphoreType.DMA((BRANCH,)),
        ],
        compiler_params=pltpu.CompilerParams(vmem_limit_bytes=32 << 20),
        name="downward",
    )(*arrived, tr, basis.reshape(nleaf * rank, points))


def solution(mesh):
    placed = (
        P(("grp", "wide"), None),
        P(("grp", "wide"), None, None),
        P(("grp", "wide")),
        P(("grp", "wide")),
        P(("grp", "wide")),
        P(("grp", "wide"), None, None),
        P(("grp", "wide"), None, None),
    )
    return jax.shard_map(
        on_device, mesh=mesh, in_specs=placed, out_specs=P(None, ("grp", "wide")), check_vma=False
    )
```

```python
import functools

import jax
import jax.numpy as jnp
from jax import lax
from jax.experimental import pallas as pl
from jax.experimental.pallas import tpu as pltpu
from jax.sharding import PartitionSpec as P

BRANCH = 8
RANK = 64
RHS = 8
SLOTS = 8
CROSS = (3,)
HALF = 4
BF = jnp.bfloat16
F32 = jnp.float32


def split(x):
    high = x.astype(BF)
    low = (x - high.astype(F32)).astype(BF)
    return high, low


def mm(a, b):
    return jnp.dot(a, b, preferred_element_type=F32)


def product3(x, weights):
    rows, columns = x.shape[0], weights.shape[1] // 2
    both = mm(jnp.concatenate(split(x), axis=0), weights)
    return both[:rows, :columns] + (both[:rows, columns:] + both[rows:, :columns])


def iota(shape, dim):
    return lax.broadcasted_iota(jnp.int32, shape, dim)


CHUNKS = 4


def prepare(coupling_in, transfer_in, ct, tr, coupling, transfer, turned, sems):
    nwide = ct.shape[0]
    ncl = transfer.shape[2]

    def chunks(source, held, at):
        size = held.shape[0] // CHUNKS
        return [
            pltpu.make_async_copy(source.at[pl.ds(size * k, size)], held.at[pl.ds(size * k, size)], sems.at[at + k])
            for k in range(CHUNKS)
        ]

    first, second = chunks(transfer_in, transfer, 0), chunks(coupling_in, coupling, CHUNKS)
    for copy in first + second:
        copy.start()

    for i in range(RANK):
        if i % (RANK // CHUNKS) == 0:
            first[i // (RANK // CHUNKS)].wait()
        turned[ncl * i : ncl * (i + 1), :] = transfer[i].T
    for g in range(1 + BRANCH):
        rows = [turned[pl.ds(BRANCH * g + c, RANK, stride=ncl), :] for c in range(BRANCH)]
        high, low = split(jnp.concatenate(rows, axis=0).T)
        tr[RANK * g : RANK * (g + 1), : BRANCH * RANK] = high
        tr[RANK * g : RANK * (g + 1), BRANCH * RANK :] = low

    def turn(p, carry):
        for s in range(HALF):
            pair = jnp.concatenate([coupling[SLOTS * p + s], coupling[SLOTS * p + HALF + s]], axis=0)
            high, low = split(pair.T)
            ct[p, RANK * s : RANK * (s + 1), :128] = high
            ct[p, RANK * s : RANK * (s + 1), 128:] = low
        return carry

    for k in range(CHUNKS):
        second[k].wait()
        lax.fori_loop(nwide // CHUNKS * k, nwide // CHUNKS * (k + 1), turn, 0, unroll=2)


def pick(two_step, source, target, counts, *refs):
    tables, (early, code, rows) = refs[:-3], refs[-3:]
    nmember, ncl = rows.shape[:2]
    nmember = nmember + 1 if two_step else nmember
    grp = lax.axis_index("grp")
    for k, table in enumerate(tables):
        rows[k] = table[...]
    if two_step:
        rows[2] = jnp.zeros(rows.shape[1:], F32)
    for b in range(early.shape[0]):
        at = source[b]
        member = sum(jnp.where(at >= ncl * k, 1, 0) for k in range(1, nmember))
        if two_step:
            apart = member ^ grp
            table = jnp.where(apart == 0, 0, jnp.where(apart == 3, 1, 2))
        else:
            table = lax.rem(grp - member + nmember, nmember)
        early[b : b + 1, :] = rows[table, pl.ds(at - ncl * member, 1), :]
    row, lane = iota((8, 128), 0), iota((8, 128), 1)
    for p in range(code.shape[0]):
        value = jnp.zeros((8, 128), jnp.int32)
        for slot in range(SLOTS):
            here = (row == slot // HALF) & ((lane % 32) // RHS == slot % HALF)
            at = jnp.where(slot < counts[p], target[SLOTS * p + slot] * RHS, -RHS)
            value = jnp.where(here, at + lane % RHS, value)
        code[p] = value.astype(F32)


def relay(theirs, own, far, out):
    ncl, width = own.shape
    grp = lax.axis_index("grp")
    row = iota((128, theirs.shape[1]), 0)
    hot = jnp.concatenate([theirs[...] - ncl * grp == row, theirs[...] - ncl * (grp ^ 3) == row], axis=0)
    hot = jnp.where(hot, 1.0, 0.0).T.astype(BF)
    none = jnp.zeros((128 - ncl, width), F32)
    high, low = split(jnp.concatenate([own[...], none, far[...], none], axis=0))
    out[...] = mm(hot, high) + mm(hot, low)


def couple(two_step, parts, *refs):
    early, (ct, code, out, held_a, held_b) = refs[:parts], refs[parts:]
    nblocks, width = early[0].shape
    wide = lax.axis_index("wide") if two_step else 0
    picked = sum(part[...] for part in early)
    place, to = iota((width, 256), 0), iota((width, 256), 1)
    turn = (place // RHS == to % RANK) & (place % RHS // 2 == to // RANK)
    turn = jnp.where(turn, 1.0, 0.0).astype(BF)
    odd = iota((nblocks, width), 1) % 2
    high, low = split(jnp.concatenate([jnp.where(odd == i, picked, 0.0) for i in range(2)], axis=0))
    turned = mm(jnp.concatenate([high, low], axis=0), turn)
    turned = turned[: 2 * nblocks] + turned[2 * nblocks :]
    first = iota((nblocks, 128), 1) < RANK
    own = iota((nblocks, 128), 0) % HALF - iota((nblocks, 128), 1) // RANK
    for s in range(4):
        for i in range(2):
            x = turned[nblocks * i : nblocks * (i + 1), 128 * (s // 2) : 128 * (s // 2 + 1)]
            swapped = pltpu.roll(x, RANK, 1)
            x = jnp.where(first, x, swapped) if s % 2 == 0 else jnp.where(first, swapped, x)
            rows = pl.ds(2 * s + i, nblocks, stride=RHS)
            held_a[rows, :] = jnp.where(own == 0, x, 0.0)
            held_b[rows, :] = jnp.where(own == 2, x, 0.0)
    messages(range(out.shape[0]), wide, CROSS if two_step else (), held_a, held_b, ct, code, [out.at[c] for c in range(out.shape[0])])


def messages(chips, wide, cross, held_a, held_b, ct, code, outs):
    left = iota((32, 128), 1) < RANK
    for chip, out in zip(chips, outs):
        for i in range(2):
            peer = (2 * chip + (1 - i if chip in cross else i)) ^ wide
            at = pl.ds(pl.multiple_of(peer * 64, 64), 64)
            z = product3(jnp.concatenate([held_a[at, :], held_b[at, :]], axis=1), ct[peer])
            out[32 * i : 32 * (i + 1), :] = jnp.where(left, z[:32], z[32:])
        peer = (2 * chip + (chip in cross)) ^ wide
        out[64:, :] = code[peer] + pltpu.roll(code[peer ^ 1], 2, 0)


def downward(kinds, *refs):
    nwide = len(kinds)
    arrived, (tr, basis, out, full, held, sems) = refs[:nwide], refs[nwide:]
    value = jnp.concatenate([message[at : at + 32, :] for message, (at, _) in zip(arrived, kinds)], axis=0)
    high, low = split(value)
    weights = jnp.concatenate([high, low], axis=1)
    lane = iota((1, 128), 1)
    codes = []
    for h in range(2):
        parts = []
        for q in range(nwide // 4):
            part = None
            for e in range(4):
                at = kinds[4 * q + e][1] + h
                row = arrived[4 * q + e][at : at + 1, :]
                part = row if part is None else jnp.where(lane // 32 == e, row, part)
            parts.append(part)
        codes.append(jnp.concatenate(parts, axis=1).astype(jnp.int32))
    rows = full.shape[0]
    place = iota((rows, 32 * nwide), 0)
    sums = []
    for h in range(2):
        r = mm(jnp.where(place == codes[h], 1.0, 0.0).astype(BF), weights)
        sums.append(r[:, :128] + r[:, 128:])
    s = jnp.where(iota((rows, 128), 1) < RANK, sums[0], sums[1])
    full[...] = s + pltpu.roll(s, RANK, 1)

    first = iota((RHS, 128), 1) < RANK

    def pairs(cluster, count):
        parts = []
        for i in range(0, count, 2):
            a = full[RHS * (cluster + i) : RHS * (cluster + i + 1), :]
            b = full[RHS * (cluster + i + 1) : RHS * (cluster + i + 2), :]
            parts.append(jnp.where(first, a, b))
        return jnp.concatenate(parts, axis=1)

    diagonal = iota((32, 256), 0) // RHS == iota((32, 256), 1) // RANK

    def spread(x):
        return jnp.where(diagonal, jnp.concatenate([x] * 4, axis=0), 0.0)

    copies = []
    top = full[:RHS, :RANK]
    middle = pairs(1, BRANCH) + product3(top, tr[:RANK, :])
    for g in range(2):
        at = slice(RANK + 256 * g, RANK + 256 * (g + 1))
        down = product3(spread(middle[:, 256 * g : 256 * (g + 1)]), tr[at, :])
        for c4 in range(4):
            c = 4 * g + c4
            leaves = pairs(1 + BRANCH + BRANCH * c, BRANCH) + down[RHS * c4 : RHS * (c4 + 1), :]
            for half in range(2):
                j = BRANCH * c + 4 * half
                rows = slice(RANK * j, RANK * (j + 4))
                far = product3(spread(leaves[:, 256 * half : 256 * (half + 1)]), jnp.concatenate(split(basis[rows, :]), axis=1))
                for l4 in range(4):
                    held[:, 128 * (j + l4) : 128 * (j + l4 + 1)] = far[RHS * l4 : RHS * (l4 + 1), :]
            at = pl.ds(128 * BRANCH * c, 128 * BRANCH)
            copies.append(pltpu.make_async_copy(held.at[:, at], out.at[:, at], sems.at[c]))
            copies[-1].start()
    for copy in copies:
        copy.wait()


VMEM = pl.BlockSpec(memory_space=pltpu.VMEM)
SMEM = pl.BlockSpec(memory_space=pltpu.SMEM)
ANY = pl.BlockSpec(memory_space=pl.ANY)


def on_device(coeff_in, coupling, source, target, counts, transfer, basis):
    nwide, ngrp = lax.axis_size("wide"), lax.axis_size("grp")
    nblocks = coupling.shape[0]
    ncl, width = coeff_in.shape
    nleaf, rank, points = basis.shape
    two_step = ngrp == 4 and nwide == 8

    shape = jax.ShapeDtypeStruct
    ct = shape((nwide, 4 * rank, 4 * rank), BF)
    tr = shape(((1 + BRANCH) * rank, 2 * BRANCH * rank), BF)
    turned = jnp.transpose(transfer, (1, 2, 0))
    ct, tr = pl.pallas_call(
        prepare,
        out_shape=(ct, tr),
        in_specs=[ANY, ANY],
        out_specs=(VMEM,) * 2,
        scratch_shapes=[
            pltpu.VMEM(coupling.shape, F32),
            pltpu.VMEM(turned.shape, F32),
            pltpu.VMEM((rank * (ncl - 1), rank), F32),
            pltpu.SemaphoreType.DMA((2 * CHUNKS,)),
        ],
        compiler_params=pltpu.CompilerParams(vmem_limit_bytes=50 << 20),
        cost_estimate=pl.CostEstimate(flops=0, bytes_accessed=10 << 20, transcendentals=0),
        name="prepare",
    )(coupling, turned)

    def moved(x, axis, n, to):
        return lax.ppermute(x, axis, [(i, to(i)) for i in range(n)])

    if two_step:
        far = moved(coeff_in, "grp", ngrp, lambda i: i ^ 3)
        theirs = moved(source, "grp", ngrp, lambda i: i ^ 1)
        far, theirs = lax.optimization_barrier((far, theirs))
        far, ct = lax.optimization_barrier((far, ct))
        across = pl.pallas_call(
            relay,
            out_shape=shape((nblocks, width), F32),
            in_specs=[VMEM] * 3,
            out_specs=VMEM,
            compiler_params=pltpu.CompilerParams(vmem_limit_bytes=16 << 20),
            name="relay",
        )(theirs.reshape(1, nblocks), coeff_in, far)
        across = moved(across, "grp", ngrp, lambda i: i ^ 1)
        tables = [coeff_in, far]
    else:
        tables = [coeff_in]
        for k in range(1, ngrp):
            tables.append(moved(coeff_in, "grp", ngrp, lambda i: (i + k) % ngrp))

    held = (3 if two_step else ngrp, ncl, width)
    early, code = pl.pallas_call(
        functools.partial(pick, two_step),
        out_shape=(shape((nblocks, width), F32), shape((nwide, 8, 128), F32)),
        in_specs=[SMEM] * 3 + [VMEM] * len(tables),
        out_specs=(VMEM,) * 2,
        scratch_shapes=[pltpu.VMEM(held, F32)],
        compiler_params=pltpu.CompilerParams(vmem_limit_bytes=16 << 20),
        name="pick",
    )(source, target, counts, *tables)
    picked = [early, across] if two_step else [early]

    chips = range(nwide // 2)
    out = pl.pallas_call(
        functools.partial(couple, two_step, len(picked)),
        out_shape=shape((nwide // 2, 72, 128), F32),
        in_specs=[VMEM] * (len(picked) + 2),
        out_specs=VMEM,
        scratch_shapes=[pltpu.VMEM((nblocks * RHS, 128), F32)] * 2,
        compiler_params=pltpu.CompilerParams(vmem_limit_bytes=32 << 20),
        name="couple",
    )(*picked, ct, code)

    if two_step:
        arrived = [out[0]]
        for k in (1, 2, 3):
            arrived.append(moved(out[k], "wide", nwide, lambda i: i ^ (2 * k + (k in CROSS))))
        mate = jnp.stack([x[32:] for x in arrived])
        mate = moved(mate, "wide", nwide, lambda i: i ^ 1)
        arrived = arrived + [mate[k] for k in range(4)]
        kinds = [(0, 64)] * 4 + [(0, 34)] * 4
    else:
        pairs = jnp.stack([out[c] for c in chips])
        single = jnp.stack([pairs[:, :32], pairs[:, 32:64]], axis=1)
        codes = jnp.stack([pairs[:, 64:], jnp.roll(pairs[:, 64:], -2, axis=1)], axis=1)
        payload = jnp.concatenate([single, codes], axis=2).reshape(nwide, 40, 128)
        payload = lax.all_to_all(payload, "wide", split_axis=0, concat_axis=0, tiled=True)
        arrived = [payload[p] for p in range(nwide)]
        kinds = [(0, 32)] * nwide

    return pl.pallas_call(
        functools.partial(downward, kinds),
        out_shape=shape((RHS, nleaf * points), F32),
        in_specs=[VMEM] * (len(arrived) + 2),
        out_specs=ANY,
        scratch_shapes=[
            pltpu.VMEM((ncl * RHS, 128), F32),
            pltpu.VMEM((RHS, nleaf * points), F32),
            pltpu.SemaphoreType.DMA((BRANCH,)),
        ],
        compiler_params=pltpu.CompilerParams(vmem_limit_bytes=32 << 20),
        name="downward",
    )(*arrived, tr, basis.reshape(nleaf * rank, points))


def solution(mesh):
    placed = (
        P(("grp", "wide"), None),
        P(("grp", "wide"), None, None),
        P(("grp", "wide")),
        P(("grp", "wide")),
        P(("grp", "wide")),
        P(("grp", "wide"), None, None),
        P(("grp", "wide"), None, None),
    )
    return jax.shard_map(
        on_device, mesh=mesh, in_specs=placed, out_specs=P(None, ("grp", "wide")), check_vma=False
    )
```

```python
import functools

import jax
import jax.numpy as jnp
from jax import lax
from jax.experimental import pallas as pl
from jax.experimental.pallas import tpu as pltpu
from jax.sharding import PartitionSpec as P

BRANCH = 8
RANK = 64
RHS = 8
SLOTS = 8
CROSS = (3,)
HALF = 4
BF = jnp.bfloat16
F32 = jnp.float32


def split(x):
    high = x.astype(BF)
    low = (x - high.astype(F32)).astype(BF)
    return high, low


def mm(a, b):
    return jnp.dot(a, b, preferred_element_type=F32)


def product3(x, weights):
    rows, columns = x.shape[0], weights.shape[1] // 2
    both = mm(jnp.concatenate(split(x), axis=0), weights)
    return both[:rows, :columns] + (both[:rows, columns:] + both[rows:, :columns])


def iota(shape, dim):
    return lax.broadcasted_iota(jnp.int32, shape, dim)


CHUNKS = 4


def prepare(coupling_in, transfer_in, ct, tr, coupling, transfer, turned, sems):
    nwide = ct.shape[0]
    ncl = transfer.shape[2]

    def chunks(source, held, at):
        size = held.shape[0] // CHUNKS
        return [
            pltpu.make_async_copy(source.at[pl.ds(size * k, size)], held.at[pl.ds(size * k, size)], sems.at[at + k])
            for k in range(CHUNKS)
        ]

    first, second = chunks(transfer_in, transfer, 0), chunks(coupling_in, coupling, CHUNKS)
    for copy in first + second:
        copy.start()

    for i in range(RANK):
        if i % (RANK // CHUNKS) == 0:
            first[i // (RANK // CHUNKS)].wait()
        turned[ncl * i : ncl * (i + 1), :] = transfer[i].T
    for g in range(1 + BRANCH):
        rows = [turned[pl.ds(BRANCH * g + c, RANK, stride=ncl), :] for c in range(BRANCH)]
        high, low = split(jnp.concatenate(rows, axis=0).T)
        tr[RANK * g : RANK * (g + 1), : BRANCH * RANK] = high
        tr[RANK * g : RANK * (g + 1), BRANCH * RANK :] = low

    def turn(p, carry):
        for s in range(HALF):
            pair = jnp.concatenate([coupling[SLOTS * p + s], coupling[SLOTS * p + HALF + s]], axis=0)
            high, low = split(pair.T)
            ct[p, RANK * s : RANK * (s + 1), :128] = high
            ct[p, RANK * s : RANK * (s + 1), 128:] = low
        return carry

    for k in range(CHUNKS):
        second[k].wait()
        lax.fori_loop(nwide // CHUNKS * k, nwide // CHUNKS * (k + 1), turn, 0, unroll=2)


def pick(two_step, source, target, counts, *refs):
    tables, (early, code, rows) = refs[:-3], refs[-3:]
    nmember, ncl = rows.shape[:2]
    nmember = nmember + 1 if two_step else nmember
    grp = lax.axis_index("grp")
    for k, table in enumerate(tables):
        rows[k] = table[...]
    if two_step:
        rows[2] = jnp.zeros(rows.shape[1:], F32)
    for b in range(early.shape[0]):
        at = source[b]
        member = sum(jnp.where(at >= ncl * k, 1, 0) for k in range(1, nmember))
        if two_step:
            apart = member ^ grp
            table = jnp.where(apart == 0, 0, jnp.where(apart == 3, 1, 2))
        else:
            table = lax.rem(grp - member + nmember, nmember)
        early[b : b + 1, :] = rows[table, pl.ds(at - ncl * member, 1), :]
    row, lane = iota((8, 128), 0), iota((8, 128), 1)
    for p in range(code.shape[0]):
        value = jnp.zeros((8, 128), jnp.int32)
        for slot in range(SLOTS):
            here = (row == slot // HALF) & ((lane % 32) // RHS == slot % HALF)
            at = jnp.where(slot < counts[p], target[SLOTS * p + slot] * RHS, -RHS)
            value = jnp.where(here, at + lane % RHS, value)
        code[p] = value.astype(F32)


def relay_own(theirs, own, part, hot):
    ncl, width = own.shape
    grp = lax.axis_index("grp")
    row = iota((128, theirs.shape[1]), 0)
    mine = jnp.where(theirs[...] - ncl * grp == row, 1.0, 0.0).T.astype(BF)
    hot[...] = jnp.where(theirs[...] - ncl * (grp ^ 3) == row, 1.0, 0.0).T.astype(BF)
    high, low = split(jnp.concatenate([own[...], jnp.zeros((128 - ncl, width), F32)], axis=0))
    part[...] = mm(mine, high) + mm(mine, low)


def relay(part, hot, far, out):
    ncl, width = far.shape
    high, low = split(jnp.concatenate([far[...], jnp.zeros((128 - ncl, width), F32)], axis=0))
    out[...] = part[...] + (mm(hot[...], high) + mm(hot[...], low))


def couple(two_step, parts, *refs):
    early, (ct, code, out, held_a, held_b) = refs[:parts], refs[parts:]
    nblocks, width = early[0].shape
    wide = lax.axis_index("wide") if two_step else 0
    picked = sum(part[...] for part in early)
    place, to = iota((width, 256), 0), iota((width, 256), 1)
    turn = (place // RHS == to % RANK) & (place % RHS // 2 == to // RANK)
    turn = jnp.where(turn, 1.0, 0.0).astype(BF)
    odd = iota((nblocks, width), 1) % 2
    high, low = split(jnp.concatenate([jnp.where(odd == i, picked, 0.0) for i in range(2)], axis=0))
    turned = mm(jnp.concatenate([high, low], axis=0), turn)
    turned = turned[: 2 * nblocks] + turned[2 * nblocks :]
    first = iota((nblocks, 128), 1) < RANK
    own = iota((nblocks, 128), 0) % HALF - iota((nblocks, 128), 1) // RANK
    for s in range(4):
        for i in range(2):
            x = turned[nblocks * i : nblocks * (i + 1), 128 * (s // 2) : 128 * (s // 2 + 1)]
            swapped = pltpu.roll(x, RANK, 1)
            x = jnp.where(first, x, swapped) if s % 2 == 0 else jnp.where(first, swapped, x)
            rows = pl.ds(2 * s + i, nblocks, stride=RHS)
            held_a[rows, :] = jnp.where(own == 0, x, 0.0)
            held_b[rows, :] = jnp.where(own == 2, x, 0.0)
    messages(range(out.shape[0]), wide, CROSS if two_step else (), held_a, held_b, ct, code, [out.at[c] for c in range(out.shape[0])])


def messages(chips, wide, cross, held_a, held_b, ct, code, outs):
    left = iota((32, 128), 1) < RANK
    for chip, out in zip(chips, outs):
        for i in range(2):
            peer = (2 * chip + (1 - i if chip in cross else i)) ^ wide
            at = pl.ds(pl.multiple_of(peer * 64, 64), 64)
            z = product3(jnp.concatenate([held_a[at, :], held_b[at, :]], axis=1), ct[peer])
            out[32 * i : 32 * (i + 1), :] = jnp.where(left, z[:32], z[32:])
        peer = (2 * chip + (chip in cross)) ^ wide
        out[64:, :] = code[peer] + pltpu.roll(code[peer ^ 1], 2, 0)


def downward(kinds, *refs):
    nwide = len(kinds)
    arrived, (tr, basis, out, full, held, sems) = refs[:nwide], refs[nwide:]
    value = jnp.concatenate([message[at : at + 32, :] for message, (at, _) in zip(arrived, kinds)], axis=0)
    high, low = split(value)
    weights = jnp.concatenate([high, low], axis=1)
    lane = iota((1, 128), 1)
    codes = []
    for h in range(2):
        parts = []
        for q in range(nwide // 4):
            part = None
            for e in range(4):
                at = kinds[4 * q + e][1] + h
                row = arrived[4 * q + e][at : at + 1, :]
                part = row if part is None else jnp.where(lane // 32 == e, row, part)
            parts.append(part)
        codes.append(jnp.concatenate(parts, axis=1).astype(jnp.int32))
    rows = full.shape[0]
    place = iota((rows, 32 * nwide), 0)
    sums = []
    for h in range(2):
        r = mm(jnp.where(place == codes[h], 1.0, 0.0).astype(BF), weights)
        sums.append(r[:, :128] + r[:, 128:])
    s = jnp.where(iota((rows, 128), 1) < RANK, sums[0], sums[1])
    full[...] = s + pltpu.roll(s, RANK, 1)

    first = iota((RHS, 128), 1) < RANK

    def pairs(cluster, count):
        parts = []
        for i in range(0, count, 2):
            a = full[RHS * (cluster + i) : RHS * (cluster + i + 1), :]
            b = full[RHS * (cluster + i + 1) : RHS * (cluster + i + 2), :]
            parts.append(jnp.where(first, a, b))
        return jnp.concatenate(parts, axis=1)

    diagonal = iota((32, 256), 0) // RHS == iota((32, 256), 1) // RANK

    def spread(x):
        return jnp.where(diagonal, jnp.concatenate([x] * 4, axis=0), 0.0)

    copies = []
    top = full[:RHS, :RANK]
    middle = pairs(1, BRANCH) + product3(top, tr[:RANK, :])
    for g in range(2):
        at = slice(RANK + 256 * g, RANK + 256 * (g + 1))
        down = product3(spread(middle[:, 256 * g : 256 * (g + 1)]), tr[at, :])
        for c4 in range(4):
            c = 4 * g + c4
            leaves = pairs(1 + BRANCH + BRANCH * c, BRANCH) + down[RHS * c4 : RHS * (c4 + 1), :]
            for half in range(2):
                j = BRANCH * c + 4 * half
                rows = slice(RANK * j, RANK * (j + 4))
                far = product3(spread(leaves[:, 256 * half : 256 * (half + 1)]), jnp.concatenate(split(basis[rows, :]), axis=1))
                for l4 in range(4):
                    held[:, 128 * (j + l4) : 128 * (j + l4 + 1)] = far[RHS * l4 : RHS * (l4 + 1), :]
            at = pl.ds(128 * BRANCH * c, 128 * BRANCH)
            copies.append(pltpu.make_async_copy(held.at[:, at], out.at[:, at], sems.at[c]))
            copies[-1].start()
    for copy in copies:
        copy.wait()


VMEM = pl.BlockSpec(memory_space=pltpu.VMEM)
SMEM = pl.BlockSpec(memory_space=pltpu.SMEM)
ANY = pl.BlockSpec(memory_space=pl.ANY)


def on_device(coeff_in, coupling, source, target, counts, transfer, basis):
    nwide, ngrp = lax.axis_size("wide"), lax.axis_size("grp")
    nblocks = coupling.shape[0]
    ncl, width = coeff_in.shape
    nleaf, rank, points = basis.shape
    two_step = ngrp == 4 and nwide == 8

    shape = jax.ShapeDtypeStruct
    ct = shape((nwide, 4 * rank, 4 * rank), BF)
    tr = shape(((1 + BRANCH) * rank, 2 * BRANCH * rank), BF)
    turned = jnp.transpose(transfer, (1, 2, 0))
    ct, tr = pl.pallas_call(
        prepare,
        out_shape=(ct, tr),
        in_specs=[ANY, ANY],
        out_specs=(VMEM,) * 2,
        scratch_shapes=[
            pltpu.VMEM(coupling.shape, F32),
            pltpu.VMEM(turned.shape, F32),
            pltpu.VMEM((rank * (ncl - 1), rank), F32),
            pltpu.SemaphoreType.DMA((2 * CHUNKS,)),
        ],
        compiler_params=pltpu.CompilerParams(vmem_limit_bytes=50 << 20),
        cost_estimate=pl.CostEstimate(flops=0, bytes_accessed=10 << 20, transcendentals=0),
        name="prepare",
    )(coupling, turned)

    def moved(x, axis, n, to):
        return lax.ppermute(x, axis, [(i, to(i)) for i in range(n)])

    if two_step:
        far = moved(coeff_in, "grp", ngrp, lambda i: i ^ 3)
        theirs = moved(source, "grp", ngrp, lambda i: i ^ 1)
        part, hot = pl.pallas_call(
            relay_own,
            out_shape=(shape((nblocks, width), F32), shape((nblocks, 128), BF)),
            in_specs=[VMEM] * 2,
            out_specs=(VMEM,) * 2,
            compiler_params=pltpu.CompilerParams(vmem_limit_bytes=16 << 20),
            name="relay_own",
        )(theirs.reshape(1, nblocks), coeff_in)
        far, ct = lax.optimization_barrier((far, ct))
        across = pl.pallas_call(
            relay,
            out_shape=shape((nblocks, width), F32),
            in_specs=[VMEM] * 3,
            out_specs=VMEM,
            compiler_params=pltpu.CompilerParams(vmem_limit_bytes=16 << 20),
            name="relay",
        )(part, hot, far)
        across = moved(across, "grp", ngrp, lambda i: i ^ 1)
        tables = [coeff_in, far]
    else:
        tables = [coeff_in]
        for k in range(1, ngrp):
            tables.append(moved(coeff_in, "grp", ngrp, lambda i: (i + k) % ngrp))

    held = (3 if two_step else ngrp, ncl, width)
    early, code = pl.pallas_call(
        functools.partial(pick, two_step),
        out_shape=(shape((nblocks, width), F32), shape((nwide, 8, 128), F32)),
        in_specs=[SMEM] * 3 + [VMEM] * len(tables),
        out_specs=(VMEM,) * 2,
        scratch_shapes=[pltpu.VMEM(held, F32)],
        compiler_params=pltpu.CompilerParams(vmem_limit_bytes=16 << 20),
        name="pick",
    )(source, target, counts, *tables)
    picked = [early, across] if two_step else [early]

    chips = range(nwide // 2)
    out = pl.pallas_call(
        functools.partial(couple, two_step, len(picked)),
        out_shape=shape((nwide // 2, 72, 128), F32),
        in_specs=[VMEM] * (len(picked) + 2),
        out_specs=VMEM,
        scratch_shapes=[pltpu.VMEM((nblocks * RHS, 128), F32)] * 2,
        compiler_params=pltpu.CompilerParams(vmem_limit_bytes=32 << 20),
        name="couple",
    )(*picked, ct, code)

    if two_step:
        arrived = [out[0]]
        for k in (1, 2, 3):
            arrived.append(moved(out[k], "wide", nwide, lambda i: i ^ (2 * k + (k in CROSS))))
        mate = jnp.stack([x[32:] for x in arrived])
        mate = moved(mate, "wide", nwide, lambda i: i ^ 1)
        arrived = arrived + [mate[k] for k in range(4)]
        kinds = [(0, 64)] * 4 + [(0, 34)] * 4
    else:
        pairs = jnp.stack([out[c] for c in chips])
        single = jnp.stack([pairs[:, :32], pairs[:, 32:64]], axis=1)
        codes = jnp.stack([pairs[:, 64:], jnp.roll(pairs[:, 64:], -2, axis=1)], axis=1)
        payload = jnp.concatenate([single, codes], axis=2).reshape(nwide, 40, 128)
        payload = lax.all_to_all(payload, "wide", split_axis=0, concat_axis=0, tiled=True)
        arrived = [payload[p] for p in range(nwide)]
        kinds = [(0, 32)] * nwide

    return pl.pallas_call(
        functools.partial(downward, kinds),
        out_shape=shape((RHS, nleaf * points), F32),
        in_specs=[VMEM] * (len(arrived) + 2),
        out_specs=ANY,
        scratch_shapes=[
            pltpu.VMEM((ncl * RHS, 128), F32),
            pltpu.VMEM((RHS, nleaf * points), F32),
            pltpu.SemaphoreType.DMA((BRANCH,)),
        ],
        compiler_params=pltpu.CompilerParams(vmem_limit_bytes=32 << 20),
        name="downward",
    )(*arrived, tr, basis.reshape(nleaf * rank, points))


def solution(mesh):
    placed = (
        P(("grp", "wide"), None),
        P(("grp", "wide"), None, None),
        P(("grp", "wide")),
        P(("grp", "wide")),
        P(("grp", "wide")),
        P(("grp", "wide"), None, None),
        P(("grp", "wide"), None, None),
    )
    return jax.shard_map(
        on_device, mesh=mesh, in_specs=placed, out_specs=P(None, ("grp", "wide")), check_vma=False
    )
```

```python
import functools

import jax
import jax.numpy as jnp
from jax import lax
from jax.experimental import pallas as pl
from jax.experimental.pallas import tpu as pltpu
from jax.sharding import PartitionSpec as P

BRANCH = 8
RANK = 64
RHS = 8
SLOTS = 8
CROSS = (3,)
HALF = 4
BF = jnp.bfloat16
F32 = jnp.float32


def split(x):
    high = x.astype(BF)
    low = (x - high.astype(F32)).astype(BF)
    return high, low


def mm(a, b):
    return jnp.dot(a, b, preferred_element_type=F32)


def product3(x, weights):
    rows, columns = x.shape[0], weights.shape[1] // 2
    both = mm(jnp.concatenate(split(x), axis=0), weights)
    return both[:rows, :columns] + (both[:rows, columns:] + both[rows:, :columns])


def iota(shape, dim):
    return lax.broadcasted_iota(jnp.int32, shape, dim)


CHUNKS = 4


def prepare(coupling_in, transfer_in, ct, tr, coupling, transfer, turned, sems):
    nwide = ct.shape[0]
    ncl = transfer.shape[2]

    def chunks(source, held, at):
        size = held.shape[0] // CHUNKS
        return [
            pltpu.make_async_copy(source.at[pl.ds(size * k, size)], held.at[pl.ds(size * k, size)], sems.at[at + k])
            for k in range(CHUNKS)
        ]

    first, second = chunks(transfer_in, transfer, 0), chunks(coupling_in, coupling, CHUNKS)
    for copy in first + second:
        copy.start()

    for i in range(RANK):
        if i % (RANK // CHUNKS) == 0:
            first[i // (RANK // CHUNKS)].wait()
        turned[ncl * i : ncl * (i + 1), :] = transfer[i].T
    for g in range(1 + BRANCH):
        rows = [turned[pl.ds(BRANCH * g + c, RANK, stride=ncl), :] for c in range(BRANCH)]
        high, low = split(jnp.concatenate(rows, axis=0).T)
        tr[RANK * g : RANK * (g + 1), : BRANCH * RANK] = high
        tr[RANK * g : RANK * (g + 1), BRANCH * RANK :] = low

    def turn(p, carry):
        for s in range(HALF):
            pair = jnp.concatenate([coupling[SLOTS * p + s], coupling[SLOTS * p + HALF + s]], axis=0)
            high, low = split(pair.T)
            ct[p, RANK * s : RANK * (s + 1), :128] = high
            ct[p, RANK * s : RANK * (s + 1), 128:] = low
        return carry

    for k in range(CHUNKS):
        second[k].wait()
        lax.fori_loop(nwide // CHUNKS * k, nwide // CHUNKS * (k + 1), turn, 0, unroll=2)


def pick(two_step, source, target, counts, *refs):
    tables, (early, code, turn, rows) = refs[:-4], refs[-4:]
    nmember, ncl = rows.shape[:2]
    nmember = nmember + 1 if two_step else nmember
    grp = lax.axis_index("grp")
    for k, table in enumerate(tables):
        rows[k] = table[...]
    if two_step:
        rows[2] = jnp.zeros(rows.shape[1:], F32)
    for b in range(early.shape[0]):
        at = source[b]
        member = sum(jnp.where(at >= ncl * k, 1, 0) for k in range(1, nmember))
        if two_step:
            apart = member ^ grp
            table = jnp.where(apart == 0, 0, jnp.where(apart == 3, 1, 2))
        else:
            table = lax.rem(grp - member + nmember, nmember)
        early[b : b + 1, :] = rows[table, pl.ds(at - ncl * member, 1), :]
    row, lane = iota((8, 128), 0), iota((8, 128), 1)
    for p in range(code.shape[0]):
        value = jnp.zeros((8, 128), jnp.int32)
        for slot in range(SLOTS):
            here = (row == slot // HALF) & ((lane % 32) // RHS == slot % HALF)
            at = jnp.where(slot < counts[p], target[SLOTS * p + slot] * RHS, -RHS)
            value = jnp.where(here, at + lane % RHS, value)
        code[p] = value.astype(F32)
    place, to = iota(turn.shape, 0), iota(turn.shape, 1)
    same = (place // RHS == to % RANK) & (place % RHS // 2 == to // RANK)
    turn[...] = jnp.where(same, 1.0, 0.0).astype(BF)


def relay_own(theirs, own, part, hot):
    ncl, width = own.shape
    grp = lax.axis_index("grp")
    row = iota((128, theirs.shape[1]), 0)
    mine = jnp.where(theirs[...] - ncl * grp == row, 1.0, 0.0).T.astype(BF)
    hot[...] = jnp.where(theirs[...] - ncl * (grp ^ 3) == row, 1.0, 0.0).T.astype(BF)
    high, low = split(jnp.concatenate([own[...], jnp.zeros((128 - ncl, width), F32)], axis=0))
    part[...] = mm(mine, high) + mm(mine, low)


def relay(part, hot, far, out):
    ncl, width = far.shape
    high, low = split(jnp.concatenate([far[...], jnp.zeros((128 - ncl, width), F32)], axis=0))
    out[...] = part[...] + (mm(hot[...], high) + mm(hot[...], low))


def couple(two_step, parts, *refs):
    early, (turn, ct, code, out, held_a, held_b) = refs[:parts], refs[parts:]
    nblocks, width = early[0].shape
    wide = lax.axis_index("wide") if two_step else 0
    picked = sum(part[...] for part in early)
    odd = iota((nblocks, width), 1) % 2
    high, low = split(jnp.concatenate([jnp.where(odd == i, picked, 0.0) for i in range(2)], axis=0))
    turned = mm(jnp.concatenate([high, low], axis=0), turn[...])
    turned = turned[: 2 * nblocks] + turned[2 * nblocks :]
    first = iota((nblocks, 128), 1) < RANK
    own = iota((nblocks, 128), 0) % HALF - iota((nblocks, 128), 1) // RANK
    for s in range(4):
        for i in range(2):
            x = turned[nblocks * i : nblocks * (i + 1), 128 * (s // 2) : 128 * (s // 2 + 1)]
            swapped = pltpu.roll(x, RANK, 1)
            x = jnp.where(first, x, swapped) if s % 2 == 0 else jnp.where(first, swapped, x)
            rows = pl.ds(2 * s + i, nblocks, stride=RHS)
            held_a[rows, :] = jnp.where(own == 0, x, 0.0)
            held_b[rows, :] = jnp.where(own == 2, x, 0.0)
    messages(range(out.shape[0]), wide, CROSS if two_step else (), held_a, held_b, ct, code, [out.at[c] for c in range(out.shape[0])])


def messages(chips, wide, cross, held_a, held_b, ct, code, outs):
    left = iota((32, 128), 1) < RANK
    for chip, out in zip(chips, outs):
        for i in range(2):
            peer = (2 * chip + (1 - i if chip in cross else i)) ^ wide
            at = pl.ds(pl.multiple_of(peer * 64, 64), 64)
            z = product3(jnp.concatenate([held_a[at, :], held_b[at, :]], axis=1), ct[peer])
            out[32 * i : 32 * (i + 1), :] = jnp.where(left, z[:32], z[32:])
        peer = (2 * chip + (chip in cross)) ^ wide
        out[64:, :] = code[peer] + pltpu.roll(code[peer ^ 1], 2, 0)


def downward(kinds, *refs):
    nwide = len(kinds)
    arrived, (tr, basis, out, full, held, sems) = refs[:nwide], refs[nwide:]
    value = jnp.concatenate([message[at : at + 32, :] for message, (at, _) in zip(arrived, kinds)], axis=0)
    high, low = split(value)
    weights = jnp.concatenate([high, low], axis=1)
    lane = iota((1, 128), 1)
    codes = []
    for h in range(2):
        parts = []
        for q in range(nwide // 4):
            part = None
            for e in range(4):
                at = kinds[4 * q + e][1] + h
                row = arrived[4 * q + e][at : at + 1, :]
                part = row if part is None else jnp.where(lane // 32 == e, row, part)
            parts.append(part)
        codes.append(jnp.concatenate(parts, axis=1).astype(jnp.int32))
    rows = full.shape[0]
    place = iota((rows, 32 * nwide), 0)
    sums = []
    for h in range(2):
        r = mm(jnp.where(place == codes[h], 1.0, 0.0).astype(BF), weights)
        sums.append(r[:, :128] + r[:, 128:])
    s = jnp.where(iota((rows, 128), 1) < RANK, sums[0], sums[1])
    full[...] = s + pltpu.roll(s, RANK, 1)

    first = iota((RHS, 128), 1) < RANK

    def pairs(cluster, count):
        parts = []
        for i in range(0, count, 2):
            a = full[RHS * (cluster + i) : RHS * (cluster + i + 1), :]
            b = full[RHS * (cluster + i + 1) : RHS * (cluster + i + 2), :]
            parts.append(jnp.where(first, a, b))
        return jnp.concatenate(parts, axis=1)

    diagonal = iota((32, 256), 0) // RHS == iota((32, 256), 1) // RANK

    def spread(x):
        return jnp.where(diagonal, jnp.concatenate([x] * 4, axis=0), 0.0)

    copies = []
    top = full[:RHS, :RANK]
    middle = pairs(1, BRANCH) + product3(top, tr[:RANK, :])
    for g in range(2):
        at = slice(RANK + 256 * g, RANK + 256 * (g + 1))
        down = product3(spread(middle[:, 256 * g : 256 * (g + 1)]), tr[at, :])
        for c4 in range(4):
            c = 4 * g + c4
            leaves = pairs(1 + BRANCH + BRANCH * c, BRANCH) + down[RHS * c4 : RHS * (c4 + 1), :]
            for half in range(2):
                j = BRANCH * c + 4 * half
                rows = slice(RANK * j, RANK * (j + 4))
                far = product3(spread(leaves[:, 256 * half : 256 * (half + 1)]), jnp.concatenate(split(basis[rows, :]), axis=1))
                for l4 in range(4):
                    held[:, 128 * (j + l4) : 128 * (j + l4 + 1)] = far[RHS * l4 : RHS * (l4 + 1), :]
            at = pl.ds(128 * BRANCH * c, 128 * BRANCH)
            copies.append(pltpu.make_async_copy(held.at[:, at], out.at[:, at], sems.at[c]))
            copies[-1].start()
    for copy in copies:
        copy.wait()


VMEM = pl.BlockSpec(memory_space=pltpu.VMEM)
SMEM = pl.BlockSpec(memory_space=pltpu.SMEM)
ANY = pl.BlockSpec(memory_space=pl.ANY)


def on_device(coeff_in, coupling, source, target, counts, transfer, basis):
    nwide, ngrp = lax.axis_size("wide"), lax.axis_size("grp")
    nblocks = coupling.shape[0]
    ncl, width = coeff_in.shape
    nleaf, rank, points = basis.shape
    two_step = ngrp == 4 and nwide == 8

    shape = jax.ShapeDtypeStruct
    ct = shape((nwide, 4 * rank, 4 * rank), BF)
    tr = shape(((1 + BRANCH) * rank, 2 * BRANCH * rank), BF)
    turned = jnp.transpose(transfer, (1, 2, 0))
    ct, tr = pl.pallas_call(
        prepare,
        out_shape=(ct, tr),
        in_specs=[ANY, ANY],
        out_specs=(VMEM,) * 2,
        scratch_shapes=[
            pltpu.VMEM(coupling.shape, F32),
            pltpu.VMEM(turned.shape, F32),
            pltpu.VMEM((rank * (ncl - 1), rank), F32),
            pltpu.SemaphoreType.DMA((2 * CHUNKS,)),
        ],
        compiler_params=pltpu.CompilerParams(vmem_limit_bytes=50 << 20),
        cost_estimate=pl.CostEstimate(flops=0, bytes_accessed=10 << 20, transcendentals=0),
        name="prepare",
    )(coupling, turned)

    def moved(x, axis, n, to):
        return lax.ppermute(x, axis, [(i, to(i)) for i in range(n)])

    if two_step:
        far = moved(coeff_in, "grp", ngrp, lambda i: i ^ 3)
        theirs = moved(source, "grp", ngrp, lambda i: i ^ 1)
        part, hot = pl.pallas_call(
            relay_own,
            out_shape=(shape((nblocks, width), F32), shape((nblocks, 128), BF)),
            in_specs=[VMEM] * 2,
            out_specs=(VMEM,) * 2,
            compiler_params=pltpu.CompilerParams(vmem_limit_bytes=16 << 20),
            name="relay_own",
        )(theirs.reshape(1, nblocks), coeff_in)
        far, ct = lax.optimization_barrier((far, ct))
        across = pl.pallas_call(
            relay,
            out_shape=shape((nblocks, width), F32),
            in_specs=[VMEM] * 3,
            out_specs=VMEM,
            compiler_params=pltpu.CompilerParams(vmem_limit_bytes=16 << 20),
            name="relay",
        )(part, hot, far)
        across = moved(across, "grp", ngrp, lambda i: i ^ 1)
        tables = [coeff_in, far]
    else:
        tables = [coeff_in]
        for k in range(1, ngrp):
            tables.append(moved(coeff_in, "grp", ngrp, lambda i: (i + k) % ngrp))

    held = (3 if two_step else ngrp, ncl, width)
    early, code, turn = pl.pallas_call(
        functools.partial(pick, two_step),
        out_shape=(shape((nblocks, width), F32), shape((nwide, 8, 128), F32), shape((width, 256), BF)),
        in_specs=[SMEM] * 3 + [VMEM] * len(tables),
        out_specs=(VMEM,) * 3,
        scratch_shapes=[pltpu.VMEM(held, F32)],
        compiler_params=pltpu.CompilerParams(vmem_limit_bytes=16 << 20),
        name="pick",
    )(source, target, counts, *tables)
    picked = [early, across] if two_step else [early]

    chips = range(nwide // 2)
    out = pl.pallas_call(
        functools.partial(couple, two_step, len(picked)),
        out_shape=shape((nwide // 2, 72, 128), F32),
        in_specs=[VMEM] * (len(picked) + 3),
        out_specs=VMEM,
        scratch_shapes=[pltpu.VMEM((nblocks * RHS, 128), F32)] * 2,
        compiler_params=pltpu.CompilerParams(vmem_limit_bytes=32 << 20),
        name="couple",
    )(*picked, turn, ct, code)

    if two_step:
        arrived = [out[0]]
        for k in (1, 2, 3):
            arrived.append(moved(out[k], "wide", nwide, lambda i: i ^ (2 * k + (k in CROSS))))
        mate = jnp.stack([x[32:] for x in arrived])
        mate = moved(mate, "wide", nwide, lambda i: i ^ 1)
        arrived = arrived + [mate[k] for k in range(4)]
        kinds = [(0, 64)] * 4 + [(0, 34)] * 4
    else:
        pairs = jnp.stack([out[c] for c in chips])
        single = jnp.stack([pairs[:, :32], pairs[:, 32:64]], axis=1)
        codes = jnp.stack([pairs[:, 64:], jnp.roll(pairs[:, 64:], -2, axis=1)], axis=1)
        payload = jnp.concatenate([single, codes], axis=2).reshape(nwide, 40, 128)
        payload = lax.all_to_all(payload, "wide", split_axis=0, concat_axis=0, tiled=True)
        arrived = [payload[p] for p in range(nwide)]
        kinds = [(0, 32)] * nwide

    return pl.pallas_call(
        functools.partial(downward, kinds),
        out_shape=shape((RHS, nleaf * points), F32),
        in_specs=[VMEM] * (len(arrived) + 2),
        out_specs=ANY,
        scratch_shapes=[
            pltpu.VMEM((ncl * RHS, 128), F32),
            pltpu.VMEM((RHS, nleaf * points), F32),
            pltpu.SemaphoreType.DMA((BRANCH,)),
        ],
        compiler_params=pltpu.CompilerParams(vmem_limit_bytes=32 << 20),
        name="downward",
    )(*arrived, tr, basis.reshape(nleaf * rank, points))


def solution(mesh):
    placed = (
        P(("grp", "wide"), None),
        P(("grp", "wide"), None, None),
        P(("grp", "wide")),
        P(("grp", "wide")),
        P(("grp", "wide")),
        P(("grp", "wide"), None, None),
        P(("grp", "wide"), None, None),
    )
    return jax.shard_map(
        on_device, mesh=mesh, in_specs=placed, out_specs=P(None, ("grp", "wide")), check_vma=False
    )
```

```python
import functools

import jax
import jax.numpy as jnp
from jax import lax
from jax.experimental import pallas as pl
from jax.experimental.pallas import tpu as pltpu
from jax.sharding import PartitionSpec as P

BRANCH = 8
RANK = 64
RHS = 8
SLOTS = 8
CROSS = (3,)
HALF = 4
BF = jnp.bfloat16
F32 = jnp.float32


def split(x):
    high = x.astype(BF)
    low = (x - high.astype(F32)).astype(BF)
    return high, low


def mm(a, b):
    return jnp.dot(a, b, preferred_element_type=F32)


def product3(x, weights):
    rows, columns = x.shape[0], weights.shape[1] // 2
    both = mm(jnp.concatenate(split(x), axis=0), weights)
    return both[:rows, :columns] + (both[:rows, columns:] + both[rows:, :columns])


def iota(shape, dim):
    return lax.broadcasted_iota(jnp.int32, shape, dim)


CHUNKS = 4


def prepare(coupling_in, transfer_in, ct, tr, coupling, transfer, turned, sems):
    nwide = ct.shape[0]
    ncl = transfer.shape[2]

    def chunks(source, held, at):
        size = held.shape[0] // CHUNKS
        return [
            pltpu.make_async_copy(source.at[pl.ds(size * k, size)], held.at[pl.ds(size * k, size)], sems.at[at + k])
            for k in range(CHUNKS)
        ]

    first, second = chunks(transfer_in, transfer, 0), chunks(coupling_in, coupling, CHUNKS)
    for copy in first + second:
        copy.start()

    for i in range(RANK):
        if i % (RANK // CHUNKS) == 0:
            first[i // (RANK // CHUNKS)].wait()
        turned[ncl * i : ncl * (i + 1), :] = transfer[i].T
    for g in range(1 + BRANCH):
        rows = [turned[pl.ds(BRANCH * g + c, RANK, stride=ncl), :] for c in range(BRANCH)]
        high, low = split(jnp.concatenate(rows, axis=0).T)
        tr[RANK * g : RANK * (g + 1), : BRANCH * RANK] = high
        tr[RANK * g : RANK * (g + 1), BRANCH * RANK :] = low

    def turn(p, carry):
        for s in range(HALF):
            pair = jnp.concatenate([coupling[SLOTS * p + s], coupling[SLOTS * p + HALF + s]], axis=0)
            high, low = split(pair.T)
            ct[p, RANK * s : RANK * (s + 1), :128] = high
            ct[p, RANK * s : RANK * (s + 1), 128:] = low
        return carry

    for k in range(CHUNKS):
        second[k].wait()
        lax.fori_loop(nwide // CHUNKS * k, nwide // CHUNKS * (k + 1), turn, 0, unroll=2)


def pick(two_step, source, target, counts, *refs):
    tables, (early, code, rows) = refs[:-3], refs[-3:]
    nmember, ncl = rows.shape[:2]
    nmember = nmember + 1 if two_step else nmember
    grp = lax.axis_index("grp")
    for k, table in enumerate(tables):
        rows[k] = table[...]
    if two_step:
        rows[2] = jnp.zeros(rows.shape[1:], F32)
    for b in range(early.shape[0]):
        at = source[b]
        member = sum(jnp.where(at >= ncl * k, 1, 0) for k in range(1, nmember))
        if two_step:
            apart = member ^ grp
            table = jnp.where(apart == 0, 0, jnp.where(apart == 3, 1, 2))
        else:
            table = lax.rem(grp - member + nmember, nmember)
        early[b : b + 1, :] = rows[table, pl.ds(at - ncl * member, 1), :]
    row, lane = iota((8, 128), 0), iota((8, 128), 1)
    for p in range(code.shape[0]):
        value = jnp.zeros((8, 128), jnp.int32)
        for slot in range(SLOTS):
            here = (row == slot // HALF) & ((lane % 32) // RHS == slot % HALF)
            at = jnp.where(slot < counts[p], target[SLOTS * p + slot] * RHS, -RHS)
            value = jnp.where(here, at + lane % RHS, value)
        code[p] = value.astype(F32)


def relay_own(theirs, own, part, hot):
    ncl, width = own.shape
    grp = lax.axis_index("grp")
    row = iota((128, theirs.shape[1]), 0)
    mine = jnp.where(theirs[...] - ncl * grp == row, 1.0, 0.0).T.astype(BF)
    hot[...] = jnp.where(theirs[...] - ncl * (grp ^ 3) == row, 1.0, 0.0).T.astype(BF)
    high, low = split(jnp.concatenate([own[...], jnp.zeros((128 - ncl, width), F32)], axis=0))
    part[...] = mm(mine, high) + mm(mine, low)


def relay(part, hot, far, out):
    ncl, width = far.shape
    high, low = split(jnp.concatenate([far[...], jnp.zeros((128 - ncl, width), F32)], axis=0))
    out[...] = part[...] + (mm(hot[...], high) + mm(hot[...], low))


def couple(two_step, parts, *refs):
    early, (ct, code, out, held_a, held_b) = refs[:parts], refs[parts:]
    nblocks, width = early[0].shape
    wide = lax.axis_index("wide") if two_step else 0
    picked = sum(part[...] for part in early)
    place, to = iota((width, 256), 0), iota((width, 256), 1)
    turn = (place // RHS == to % RANK) & (place % RHS // 2 == to // RANK)
    turn = jnp.where(turn, 1.0, 0.0).astype(BF)
    odd = iota((nblocks, width), 1) % 2
    high, low = split(jnp.concatenate([jnp.where(odd == i, picked, 0.0) for i in range(2)], axis=0))
    turned = mm(jnp.concatenate([high, low], axis=0), turn)
    turned = turned[: 2 * nblocks] + turned[2 * nblocks :]
    first = iota((nblocks, 128), 1) < RANK
    own = iota((nblocks, 128), 0) % HALF - iota((nblocks, 128), 1) // RANK
    for s in range(4):
        for i in range(2):
            x = turned[nblocks * i : nblocks * (i + 1), 128 * (s // 2) : 128 * (s // 2 + 1)]
            swapped = pltpu.roll(x, RANK, 1)
            x = jnp.where(first, x, swapped) if s % 2 == 0 else jnp.where(first, swapped, x)
            rows = pl.ds(2 * s + i, nblocks, stride=RHS)
            held_a[rows, :] = jnp.where(own == 0, x, 0.0)
            held_b[rows, :] = jnp.where(own == 2, x, 0.0)
    messages(range(out.shape[0]), wide, CROSS if two_step else (), held_a, held_b, ct, code, [out.at[c] for c in range(out.shape[0])])


def messages(chips, wide, cross, held_a, held_b, ct, code, outs):
    left = iota((32, 128), 1) < RANK
    for chip, out in zip(chips, outs):
        for i in range(2):
            peer = (2 * chip + (1 - i if chip in cross else i)) ^ wide
            at = pl.ds(pl.multiple_of(peer * 64, 64), 64)
            z = product3(jnp.concatenate([held_a[at, :], held_b[at, :]], axis=1), ct[peer])
            out[32 * i : 32 * (i + 1), :] = jnp.where(left, z[:32], z[32:])
        peer = (2 * chip + (chip in cross)) ^ wide
        out[64:, :] = code[peer] + pltpu.roll(code[peer ^ 1], 2, 0)


def downward(kinds, *refs):
    nwide = len(kinds)
    arrived, (tr, basis, out, full, held, sems) = refs[:nwide], refs[nwide:]
    value = jnp.concatenate([message[at : at + 32, :] for message, (at, _) in zip(arrived, kinds)], axis=0)
    high, low = split(value)
    weights = jnp.concatenate([high, low], axis=1)
    lane = iota((1, 128), 1)
    codes = []
    for h in range(2):
        parts = []
        for q in range(nwide // 4):
            part = None
            for e in range(4):
                at = kinds[4 * q + e][1] + h
                row = arrived[4 * q + e][at : at + 1, :]
                part = row if part is None else jnp.where(lane // 32 == e, row, part)
            parts.append(part)
        codes.append(jnp.concatenate(parts, axis=1).astype(jnp.int32))
    rows = full.shape[0]
    place = iota((rows, 32 * nwide), 0)
    sums = []
    for h in range(2):
        r = mm(jnp.where(place == codes[h], 1.0, 0.0).astype(BF), weights)
        sums.append(r[:, :128] + r[:, 128:])
    s = jnp.where(iota((rows, 128), 1) < RANK, sums[0], sums[1])
    full[...] = s + pltpu.roll(s, RANK, 1)

    first = iota((RHS, 128), 1) < RANK

    def pairs(cluster, count):
        parts = []
        for i in range(0, count, 2):
            a = full[RHS * (cluster + i) : RHS * (cluster + i + 1), :]
            b = full[RHS * (cluster + i + 1) : RHS * (cluster + i + 2), :]
            parts.append(jnp.where(first, a, b))
        return jnp.concatenate(parts, axis=1)

    diagonal = iota((32, 256), 0) // RHS == iota((32, 256), 1) // RANK

    def spread(x):
        return jnp.where(diagonal, jnp.concatenate([x] * 4, axis=0), 0.0)

    copies = []
    top = full[:RHS, :RANK]
    middle = pairs(1, BRANCH) + product3(top, tr[:RANK, :])
    for g in range(2):
        at = slice(RANK + 256 * g, RANK + 256 * (g + 1))
        down = product3(spread(middle[:, 256 * g : 256 * (g + 1)]), tr[at, :])
        for c4 in range(4):
            c = 4 * g + c4
            leaves = pairs(1 + BRANCH + BRANCH * c, BRANCH) + down[RHS * c4 : RHS * (c4 + 1), :]
            for half in range(2):
                j = BRANCH * c + 4 * half
                rows = slice(RANK * j, RANK * (j + 4))
                far = product3(spread(leaves[:, 256 * half : 256 * (half + 1)]), jnp.concatenate(split(basis[rows, :]), axis=1))
                for l4 in range(4):
                    held[:, 128 * (j + l4) : 128 * (j + l4 + 1)] = far[RHS * l4 : RHS * (l4 + 1), :]
            at = pl.ds(128 * BRANCH * c, 128 * BRANCH)
            copies.append(pltpu.make_async_copy(held.at[:, at], out.at[:, at], sems.at[c]))
            copies[-1].start()
    for copy in copies:
        copy.wait()


VMEM = pl.BlockSpec(memory_space=pltpu.VMEM)
SMEM = pl.BlockSpec(memory_space=pltpu.SMEM)
ANY = pl.BlockSpec(memory_space=pl.ANY)


def on_device(coeff_in, coupling, source, target, counts, transfer, basis):
    nwide, ngrp = lax.axis_size("wide"), lax.axis_size("grp")
    nblocks = coupling.shape[0]
    ncl, width = coeff_in.shape
    nleaf, rank, points = basis.shape
    two_step = ngrp == 4 and nwide == 8

    shape = jax.ShapeDtypeStruct
    ct = shape((nwide, 4 * rank, 4 * rank), BF)
    tr = shape(((1 + BRANCH) * rank, 2 * BRANCH * rank), BF)
    turned = jnp.transpose(transfer, (1, 2, 0))
    ct, tr = pl.pallas_call(
        prepare,
        out_shape=(ct, tr),
        in_specs=[ANY, ANY],
        out_specs=(VMEM,) * 2,
        scratch_shapes=[
            pltpu.VMEM(coupling.shape, F32),
            pltpu.VMEM(turned.shape, F32),
            pltpu.VMEM((rank * (ncl - 1), rank), F32),
            pltpu.SemaphoreType.DMA((2 * CHUNKS,)),
        ],
        compiler_params=pltpu.CompilerParams(vmem_limit_bytes=50 << 20),
        cost_estimate=pl.CostEstimate(flops=0, bytes_accessed=10 << 20, transcendentals=0),
        name="prepare",
    )(coupling, turned)

    def moved(x, axis, n, to):
        return lax.ppermute(x, axis, [(i, to(i)) for i in range(n)])

    if two_step:
        far = moved(coeff_in, "grp", ngrp, lambda i: i ^ 3)
        theirs = moved(source, "grp", ngrp, lambda i: i ^ 1)
        part, hot = pl.pallas_call(
            relay_own,
            out_shape=(shape((nblocks, width), F32), shape((nblocks, 128), BF)),
            in_specs=[VMEM] * 2,
            out_specs=(VMEM,) * 2,
            compiler_params=pltpu.CompilerParams(vmem_limit_bytes=16 << 20),
            name="relay_own",
        )(theirs.reshape(1, nblocks), coeff_in)
        far, ct = lax.optimization_barrier((far, ct))
        across = pl.pallas_call(
            relay,
            out_shape=shape((nblocks, width), F32),
            in_specs=[VMEM] * 3,
            out_specs=VMEM,
            compiler_params=pltpu.CompilerParams(vmem_limit_bytes=16 << 20),
            name="relay",
        )(part, hot, far)
        across = moved(across, "grp", ngrp, lambda i: i ^ 1)
        tables = [coeff_in, far]
    else:
        tables = [coeff_in]
        for k in range(1, ngrp):
            tables.append(moved(coeff_in, "grp", ngrp, lambda i: (i + k) % ngrp))

    held = (3 if two_step else ngrp, ncl, width)
    early, code = pl.pallas_call(
        functools.partial(pick, two_step),
        out_shape=(shape((nblocks, width), F32), shape((nwide, 8, 128), F32)),
        in_specs=[SMEM] * 3 + [VMEM] * len(tables),
        out_specs=(VMEM,) * 2,
        scratch_shapes=[pltpu.VMEM(held, F32)],
        compiler_params=pltpu.CompilerParams(vmem_limit_bytes=16 << 20),
        name="pick",
    )(source, target, counts, *tables)
    picked = [early, across] if two_step else [early]

    chips = range(nwide // 2)
    out = pl.pallas_call(
        functools.partial(couple, two_step, len(picked)),
        out_shape=shape((nwide // 2, 72, 128), F32),
        in_specs=[VMEM] * (len(picked) + 2),
        out_specs=VMEM,
        scratch_shapes=[pltpu.VMEM((nblocks * RHS, 128), F32)] * 2,
        compiler_params=pltpu.CompilerParams(vmem_limit_bytes=32 << 20),
        name="couple",
    )(*picked, ct, code)

    if two_step:
        arrived = [out[0]]
        for k in (2, 1, 3):
            arrived.append(moved(out[k], "wide", nwide, lambda i: i ^ (2 * k + (k in CROSS))))
        mate = jnp.stack([x[32:] for x in arrived])
        mate = moved(mate, "wide", nwide, lambda i: i ^ 1)
        arrived = arrived + [mate[k] for k in range(4)]
        kinds = [(0, 64)] * 4 + [(0, 34)] * 4
    else:
        pairs = jnp.stack([out[c] for c in chips])
        single = jnp.stack([pairs[:, :32], pairs[:, 32:64]], axis=1)
        codes = jnp.stack([pairs[:, 64:], jnp.roll(pairs[:, 64:], -2, axis=1)], axis=1)
        payload = jnp.concatenate([single, codes], axis=2).reshape(nwide, 40, 128)
        payload = lax.all_to_all(payload, "wide", split_axis=0, concat_axis=0, tiled=True)
        arrived = [payload[p] for p in range(nwide)]
        kinds = [(0, 32)] * nwide

    return pl.pallas_call(
        functools.partial(downward, kinds),
        out_shape=shape((RHS, nleaf * points), F32),
        in_specs=[VMEM] * (len(arrived) + 2),
        out_specs=ANY,
        scratch_shapes=[
            pltpu.VMEM((ncl * RHS, 128), F32),
            pltpu.VMEM((RHS, nleaf * points), F32),
            pltpu.SemaphoreType.DMA((BRANCH,)),
        ],
        compiler_params=pltpu.CompilerParams(vmem_limit_bytes=32 << 20),
        name="downward",
    )(*arrived, tr, basis.reshape(nleaf * rank, points))


def solution(mesh):
    placed = (
        P(("grp", "wide"), None),
        P(("grp", "wide"), None, None),
        P(("grp", "wide")),
        P(("grp", "wide")),
        P(("grp", "wide")),
        P(("grp", "wide"), None, None),
        P(("grp", "wide"), None, None),
    )
    return jax.shard_map(
        on_device, mesh=mesh, in_specs=placed, out_specs=P(None, ("grp", "wide")), check_vma=False
    )
```
